128 devices in a mesh: row: 16 (over x, z_lo, core), col: 8 (over y, z_hi).
Axes of the slice: x: 4, y: 4, z: 4 (z_hi: 2, z_lo: 2; z = z_hi * 2 + z_lo), core: 2. Of those that a mesh axis runs over, the one named last changes fastest.
Arguments:
- built: bfloat16 [8192, 8192], P('row', 'col'), may hold values from -0.59765625 to 0.59765625
- build_order: int32 [64], replicated, may hold values from 0 to 63, each once
- p_pattern: int32 [64, 64], replicated, may hold values from 0 to 1, as said below
- q_pattern: int32 [64, 64], replicated, may hold values from 0 to 1, as said below
Outputs:
- purified: bfloat16 [8192, 8192], P('row', 'col')
The draws below stay inside these ranges and needn't reach their ends.
Inputs may be any that keep to these rules, and one draw needn't show every extreme that they name: p_pattern is symmetric and 1 on the diagonal; p_pattern[i, j] is 0 unless the distance of i and j counted round the 64 blocks, or that of i and j + 32, is at most 1. q_pattern[i, j] is 0 unless the distance of i and j counted round the 64 blocks, or that of i and j + 32, is at most 2.
All inputs are finite; a program needn't handle non-finite values.
Results may differ from the reference program's by a relative error of at most 0.0045.
Values may be sent and summed in bfloat16 or wider, within the bound.
No kernel may reach another device: no remote copies, remote signals or barrier semaphores. Data moves between devices by JAX's collectives and lax.ppermute only.
A program may use at most 128 MiB of HBM per device.

```python
import jax
import jax.numpy as jnp

BS = 128
HW = 1
NB = 64


def round_distance(diff):
    wrapped = jnp.mod(diff, NB)
    return jnp.minimum(wrapped, NB - wrapped)


def block_layout(key):
    base = jax.random.fold_in(key, 41)
    side_y = jax.random.randint(jax.random.fold_in(base, 2), (NB,), 0, 3)
    side_z = jax.random.randint(jax.random.fold_in(base, 3), (NB,), 0, 3)
    index = jnp.arange(NB, dtype=jnp.int32)
    diff = index[:, None] - index[None, :]
    direct = round_distance(diff)
    across = round_distance(diff - NB // 2)
    steps_apart = jnp.minimum(direct, across)
    side_sq = (side_y[:, None] - side_y[None, :]) ** 2 + (side_z[:, None] - side_z[None, :]) ** 2
    stored = jnp.logical_and(steps_apart <= HW, side_sq + 4 * steps_apart * steps_apart <= 8).astype(jnp.int32)
    reach = jnp.dot(stored, stored) > 0
    kept = jnp.logical_and(reach, jnp.logical_and(steps_apart <= 2 * HW, side_sq + 4 * steps_apart * steps_apart <= 20)).astype(jnp.int32)
    return (stored, kept)


def draw_p_pattern(key, part):
    return block_layout(key)[0]


def draw_q_pattern(key, part):
    return block_layout(key)[1]


def block_levels(rng, dims, shards, smallest, high):
    def one(position, shards_of):
        steps = jax.random.uniform(jax.random.fold_in(jax.random.fold_in(rng, 6), position), (shards_of,), jnp.float32, smallest / len(shards), high / len(shards))
        return jnp.repeat(jnp.exp(steps), dims[position] // shards_of).reshape((-1,) + (1,) * (len(dims) - position - 1))

    level = one(*shards[0])
    for cut in shards[1:]:
        level = level * one(*cut)
    return level


def gaussian(rng, shape, deviation, limit, cuts=(), kind=jnp.bfloat16):
    level = block_levels(rng, shape, cuts, -0.22, 0.18) if cuts else 1.0
    drawn = jax.random.normal(rng, shape, jnp.float32) * deviation * level
    return jnp.minimum(jnp.maximum(drawn, -limit), limit).astype(kind)


def setup_inputs(seed: int = 0) -> dict:
    seeds = jax.random.split(jax.random.key(seed), 5)
    built = gaussian(seeds[0], (NB * BS, NB * BS), 0.1, 0.59765625, ((0, 16), (1, 8)))
    build_order = jax.random.permutation(seeds[1], NB).astype(jnp.int32)
    p_pattern = draw_p_pattern(jax.random.fold_in(seeds[4], 71), 0)
    q_pattern = draw_q_pattern(jax.random.fold_in(seeds[4], 71), 0)
    return {"built": built, "build_order": build_order, "p_pattern": p_pattern, "q_pattern": q_pattern}


def place_rows(built, build_order):
    blocks = built.reshape(NB, BS, NB * BS)
    placed = jnp.zeros_like(blocks).at[build_order].set(blocks)
    return placed.reshape(NB * BS, NB * BS)


def apply_blocks(matrix, pattern):
    shaped = matrix.reshape(NB, BS, NB, BS)
    return (shaped * pattern.astype(matrix.dtype)[:, None, :, None]).reshape(NB * BS, NB * BS)


def reference(built, build_order, p_pattern, q_pattern):
    density = apply_blocks(place_rows(built, build_order), p_pattern)
    square = apply_blocks(jnp.dot(density, density, preferred_element_type=jnp.float32), q_pattern)
    rounded = square.astype(jnp.bfloat16)
    cubed_term = jnp.dot(rounded, density, preferred_element_type=jnp.float32)
    result = apply_blocks(3.0 * square - 2.0 * cubed_term, q_pattern)
    return result.astype(jnp.bfloat16)
```

```python
import functools

import jax
import jax.numpy as jnp
import numpy as np
from jax import lax
from jax.experimental import pallas as pl
from jax.experimental.pallas import tpu as pltpu
from jax.sharding import Mesh
from jax.sharding import PartitionSpec as P

BS = 128
GRID = (4, 2, 2, 2, 2, 2)
AXES = ("x", "zl", "core", "yh", "yl", "zh")
ROW = ("x", "zl", "core")
COL = ("yh", "yl", "zh")
CHIPS = 8
PART = BS // CHIPS
WIN = 13
PLACES = [(b + e, b) for b in range(-2, 3) for e in (-1, 0, 1) if abs(b + e) <= 2]
SLOT = {rc: n for n, rc in enumerate(PLACES)}

VMEM = pl.BlockSpec(memory_space=pltpu.VMEM)
SMEM = pl.BlockSpec(memory_space=pltpu.SMEM)
HBM = pl.BlockSpec(memory_space=pl.ANY)
PARAMS = pltpu.CompilerParams(vmem_limit_bytes=48 * 1024 * 1024)


def chip_index():
    return lax.axis_index("x") * 2 + lax.axis_index("zl")


def group_index():
    return lax.axis_index("yl") * 2 + lax.axis_index("zh")


def pick_kernel(order, built, out, sem):
    first = (chip_index() * 2 + lax.axis_index("core")) * 4
    copies = []
    for k in range(4):
        row = order[first + k]
        for d in range(3):
            col = lax.rem(row + d + 31, 8)
            at = pl.ds(pl.multiple_of(col * BS, BS), BS)
            copies.append(
                pltpu.make_async_copy(
                    built.at[k, :, :, at], out.at[:, 3 * k + d], sem.at[3 * k + d]
                )
            )
            copies[-1].start()
    for copy in copies:
        copy.wait()


def place_kernel(order, pattern, mine, other, out, inverse):
    for k in range(64):
        inverse[order[k]] = k
    core = lax.axis_index("core")
    yh = lax.axis_index("yh")
    base = group_index() * 8
    for bl in range(8):
        for e in range(3):
            row = lax.rem(base + bl + e + 31, 32) + 32 * core
            at = inverse[row]
            device = at // 4
            slot = lax.rem(at, 4) * 3 + (2 - e)
            chip = device // 2
            here = lax.rem(device, 2) == core
            keep = pattern[row, base + bl + 32 * yh] != 0
            value = jnp.where(here, mine[chip, slot], other[chip, slot])
            out[3 * bl + e] = jnp.where(keep, value, jnp.zeros_like(value))


def window_kernel(left, own, right, out):
    def piece(first, last):
        for ref, lo, hi in ((left, 0, 5), (own, 5, 29), (right, 29, 34)):
            a, b = max(first, lo), min(last, hi)
            if a < b:
                yield a, b, ref[a - lo : b - lo]

    for q in range(CHIPS):
        for a, b, value in piece(3 * q, 3 * q + WIN):
            for half in range(2):
                out[2 * q + half, a - 3 * q : b - 3 * q] = value


def purify_kernel(pattern, mine, other, rows_out, near_out, far_out, blocks):
    core = lax.axis_index("core")
    yh = lax.axis_index("yh")
    q = chip_index()
    middle = group_index() * 8 + q
    for n in range(WIN):
        for chip in range(CHIPS):
            for half in range(2):
                at = pl.ds(chip * PART, PART)
                blocks[n, half, core, at] = mine[2 * chip + half, n]
                blocks[n, half, 1 - core, at] = other[2 * chip + half, n]

    def whole(row, col):
        n = SLOT[row, col]
        return jnp.concatenate(
            [blocks[n, 0].reshape(2 * BS, BS), blocks[n, 1].reshape(2 * BS, BS)], 1
        )

    def left(col):
        n = SLOT[0, col]
        return jnp.concatenate([blocks[n, 0, core], blocks[n, 1, core]], 1)

    def dot(a, b):
        return jnp.dot(a, b, preferred_element_type=jnp.float32)

    row = middle + 32 * core
    squares, rounded = [], []
    for k in range(-2, 3):
        total = None
        for l in range(-1, 2):
            if abs(l - k) <= 1:
                term = dot(left(l), whole(l, k))
                total = term if total is None else total + term
        col = lax.rem(middle + k + 32, 32)
        halves = []
        for half in range(2):
            part = total[:, half * BS : (half + 1) * BS]
            keep = pattern[row, col + 32 * half] != 0
            halves.append(jnp.where(keep, part, jnp.zeros_like(part)))
        squares.append(jnp.where(yh == 0, halves[0], halves[1]))
        rounded.append(jnp.concatenate(halves, 1).astype(jnp.bfloat16))
    results = []
    for j in range(-2, 3):
        total = None
        for k in range(-2, 3):
            if abs(k - j) <= 1:
                term = dot(rounded[k + 2], blocks[SLOT[k, j], yh].reshape(2 * BS, BS))
                total = term if total is None else total + term
        col = lax.rem(middle + j + 32, 32)
        keep = pattern[row, col + 32 * yh] != 0
        value = 3.0 * squares[j + 2] - 2.0 * total
        results.append(jnp.where(keep, value, jnp.zeros_like(value)).astype(jnp.bfloat16))
        rows_out[j + 2] = results[-1]
    low = q < 4
    near_out[0] = jnp.where(low, results[0], results[3])
    near_out[1] = jnp.where(low, results[1], results[4])
    far_out[0] = jnp.where(low, results[0], results[4])


def output_kernel(r0, r1, r2, r3, near, far, out):
    out[...] = jnp.zeros_like(out)
    core = lax.axis_index("core")
    away = lax.rem(chip_index() - group_index() + 8, 4)

    def put(row, col, value):
        out[row * BS : (row + 1) * BS, col * BS : (col + 1) * BS] = value

    for u in range(2):

        @pl.when(jnp.logical_and(away == 0, core == u))
        def _(u=u):
            for s, ref in enumerate((r0, r1, r2, r3)):
                for n in range(5):
                    col = 4 * u + s + n - 2
                    if 0 <= col < 8:
                        put(s, col, ref[n])

    @pl.when(jnp.logical_and(away == 1, core == 0))
    def _():
        put(0, 6, near[0])
        put(0, 7, near[1])
        put(1, 7, far[0])

    @pl.when(jnp.logical_and(away == 3, core == 1))
    def _():
        put(2, 0, far[0])
        put(3, 0, near[0])
        put(3, 1, near[1])


def device(q, core, yh, g):
    return ((q * 2 + core) * 2 + yh) * 4 + g % 4


PLANES = [(core, yh, g) for core in range(2) for yh in range(2) for g in range(4)]


def to_rows(s):
    return [
        (device(4 * u + s, core, yh, g), device(g + 4 * core, u, yh, g))
        for core, yh, g in PLANES
        for u in range(2)
    ]


def to_corners(low, high):
    return [
        (device(q, core, yh, g), device(g + 4 * core, u, yh, g + step))
        for core, yh, g in PLANES
        for q, u, step in ((low, 0, -1), (high, 1, 1))
    ]


def call(kernel, shape, specs, out_spec=VMEM, scratch=()):
    make = lambda s: jax.ShapeDtypeStruct(s, jnp.bfloat16)
    many = isinstance(shape, list)
    return pl.pallas_call(
        kernel,
        out_shape=[make(s) for s in shape] if many else make(shape),
        in_specs=specs,
        out_specs=[out_spec] * len(shape) if many else out_spec,
        scratch_shapes=list(scratch),
        compiler_params=PARAMS,
    )


def swap_cores(a):
    return lax.ppermute(a, "core", [(0, 1), (1, 0)])


def body(built, build_order, p_pattern, q_pattern):
    parts = call(
        pick_kernel,
        (CHIPS, 12, PART, BS),
        [SMEM, HBM],
        HBM,
        [pltpu.SemaphoreType.DMA((12,))],
    )(build_order, built.reshape(4, CHIPS, PART, 8 * BS))
    parts = lax.all_to_all(parts, ("x", "zl"), 0, 0, tiled=True)
    placed = call(
        place_kernel,
        (24, PART, BS),
        [SMEM, SMEM, VMEM, VMEM],
        scratch=[pltpu.SMEM((64,), jnp.int32)],
    )(build_order, p_pattern, parts, swap_cores(parts))
    right_of = [(g, (g + 1) % 4) for g in range(4)]
    left = lax.ppermute(placed[19:], ("yl", "zh"), right_of)
    right = lax.ppermute(placed[:5], ("yl", "zh"), [(b, a) for a, b in right_of])
    windows = call(window_kernel, (2 * CHIPS, WIN, PART, BS), [VMEM] * 3)(left, placed, right)
    windows = lax.all_to_all(windows, ("x", "zl", "yh"), 0, 0, tiled=True)
    rows, near, far = call(
        purify_kernel,
        [(5, BS, BS), (2, BS, BS), (1, BS, BS)],
        [SMEM, VMEM, VMEM],
        scratch=[pltpu.VMEM((WIN, 2, 2, BS, BS), jnp.bfloat16)],
    )(q_pattern, windows, swap_cores(windows))
    near = lax.ppermute(near, AXES, to_corners(0, 7))
    far = lax.ppermute(far, AXES, to_corners(1, 6))
    sent = [lax.ppermute(rows, AXES, to_rows(s)) for s in range(4)]
    return call(output_kernel, (4 * BS, 8 * BS), [VMEM] * 6)(*sent, near, far)


def solution(mesh):
    fine = Mesh(mesh.devices.reshape(GRID), AXES)
    placed = (P(ROW, COL), P(), P(), P())
    return jax.shard_map(
        body, mesh=fine, in_specs=placed, out_specs=P(ROW, COL), check_vma=False
    )
```

```python
import functools

import jax
import jax.numpy as jnp
import numpy as np
from jax import lax
from jax.experimental import pallas as pl
from jax.experimental.pallas import tpu as pltpu
from jax.sharding import Mesh
from jax.sharding import PartitionSpec as P

BS = 128
GRID = (4, 2, 2, 2, 2, 2)
AXES = ("x", "zl", "core", "yh", "yl", "zh")
ROW = ("x", "zl", "core")
COL = ("yh", "yl", "zh")
CHIPS = 8
PART = BS // CHIPS
WIDE = 34
WIN = 28
STARTS = (3, 6, 3, 0)

VMEM = pl.BlockSpec(memory_space=pltpu.VMEM)
SMEM = pl.BlockSpec(memory_space=pltpu.SMEM)
HBM = pl.BlockSpec(memory_space=pltpu.HBM)
PARAMS = pltpu.CompilerParams(vmem_limit_bytes=48 * 1024 * 1024)


def chip_index():
    return lax.axis_index("x") * 2 + lax.axis_index("zl")


def group_index():
    return lax.axis_index("yl") * 2 + lax.axis_index("zh")


def pick_kernel(order, built, out, order_s, built_v, sem):
    copies = [
        pltpu.make_async_copy(order, order_s, sem.at[0]),
        pltpu.make_async_copy(built, built_v, sem.at[1]),
    ]
    for copy in copies:
        copy.start()
    for copy in copies:
        copy.wait()
    first = (chip_index() * 2 + lax.axis_index("core")) * 4
    zh = lax.axis_index("zh")
    for k in range(4):
        row = order_s[first + k]
        for d in range(3):
            col = lax.rem(row + d + 31, 8)
            at = pl.ds(pl.multiple_of(col * BS, BS), BS)
            for chip in range(0, CHIPS, 2):
                out[chip, 3 * k + d] = built_v[k, chip + zh, :, at]
                out[chip + 1, 3 * k + d] = built_v[k, chip + 1 - zh, :, at]


def place_kernel(order, pattern, mine, other, out, inverse):
    for k in range(64):
        inverse[order[k]] = k
    core = lax.axis_index("core")
    yh = lax.axis_index("yh")
    base = group_index() * 8
    for bl in range(8):
        for e in range(3):
            row = lax.rem(base + bl + e + 31, 32) + 32 * core
            at = inverse[row]
            device = at // 4
            slot = lax.rem(at, 4) * 3 + (2 - e)
            chip = device // 2
            here = lax.rem(device, 2) == core
            keep = pattern[row, base + bl + 32 * yh] != 0
            value = jnp.where(here, mine[chip, slot], other[chip, slot])
            out[3 * bl + e] = jnp.where(keep, value, jnp.zeros_like(value))


def distance(chip):
    return lax.rem(chip - group_index() + 8, 4)


def window_kernel(left, own, right, out, wide):
    wide[:5] = left[...]
    wide[5:29] = own[...]
    wide[29:] = right[...]
    for chip in range(CHIPS):
        away = distance(chip)
        start = jnp.where(away == 1, STARTS[1], jnp.where(away == 3, STARTS[3], STARTS[0]))
        value = wide[pl.ds(start, WIN)]
        for half in range(2):
            out[2 * chip + half] = value


def purify_kernel(pattern, mine, other, out, squares, rounded):
    core = lax.axis_index("core")
    yh = lax.axis_index("yh")
    zh = lax.axis_index("zh")
    chip = chip_index()
    away = distance(chip)
    row_half = chip // 4
    base = group_index() * 8
    out[...] = jnp.zeros_like(out)

    def dot(a, b):
        return jnp.dot(a, b, preferred_element_type=jnp.float32)

    def block(ref, n, half):
        rows = [ref[2 * (p + zh if p % 2 == 0 else p - zh) + half, n] for p in range(CHIPS)]
        return jnp.concatenate(rows, 0)

    def kept(row, col, half):
        i = lax.rem(base + row + 32, 32) + 32 * row_half
        j = lax.rem(base + col + 32, 32) + 32 * half
        return pattern[i, j] != 0

    def work(u, start, rows, results):
        halves = (mine, other) if u == 0 else (other, mine)
        same = row_half == u

        def number(row, col):
            return 2 * col + row + 6 - start

        def column(row, col, half):
            return jnp.concatenate([block(h, number(row, col), half) for h in halves], 0)

        def whole(row, col):
            return jnp.concatenate([column(row, col, half) for half in range(2)], 1)

        def left(row, col):
            n = number(row, col)
            parts = [
                jnp.where(same, block(mine, n, half), block(other, n, half)) for half in range(2)
            ]
            return jnp.concatenate(parts, 1)

        near = lambda a, b, d=1: abs(a - b) <= d
        span = range(-2, 10)
        cols = {a: sorted({k for b, j in results if b == a for k in span if near(k, j) and near(k, a, 2)}) for a in rows}
        for a in rows:
            for k in cols[a]:
                ls = [l for l in span if near(l, a) and near(l, k)]
                total = dot(
                    jnp.concatenate([left(a, l) for l in ls], 1),
                    jnp.concatenate([whole(l, k) for l in ls], 0),
                )
                at = (rows.index(a), k - cols[a][0])
                parts = []
                for half in range(2):
                    part = total[:, half * BS : (half + 1) * BS]
                    parts.append(jnp.where(kept(a, k, half), part, jnp.zeros_like(part)))
                squares[at] = jnp.where(yh == 0, parts[0], parts[1])
                rounded[at] = jnp.concatenate(parts, 1).astype(jnp.bfloat16)
        for (a, j), (r, c) in results.items():
            ks = [k for k in cols[a] if near(k, j)]
            r_at, first = rows.index(a), cols[a][0]
            total = dot(
                jnp.concatenate([rounded[r_at, k - first] for k in ks], 1),
                jnp.concatenate([column(k, j, yh) for k in ks], 0),
            )
            value = 3.0 * squares[r_at, j - first] - 2.0 * total
            value = jnp.where(kept(a, j, yh), value, jnp.zeros_like(value))
            out[r * BS : (r + 1) * BS, c * BS : (c + 1) * BS] = value.astype(jnp.bfloat16)

    for u in range(2):

        @pl.when(jnp.logical_and(away == 0, core == u))
        def _(u=u):
            rows = list(range(4 * u, 4 * u + 4))
            spots = [(a, j) for a in rows for j in range(a - 2, a + 3) if 0 <= j < 8]
            work(u, STARTS[0], rows, {(a, j): (a - 4 * u, j) for a, j in spots})

    @pl.when(jnp.logical_and(away == 1, core == 0))
    def _():
        work(0, STARTS[1], [8, 9], {(8, 6): (0, 6), (8, 7): (0, 7), (9, 7): (1, 7)})

    @pl.when(jnp.logical_and(away == 3, core == 1))
    def _():
        work(1, STARTS[3], [-1, -2], {(-1, 1): (3, 1), (-1, 0): (3, 0), (-2, 0): (2, 0)})


def to_group(step):
    return [
        (
            ((zl * 2 + g // 2) * 2) + g % 2,
            (((1 - zl) * 2 + (g + step) % 4 // 2) * 2) + (g + step) % 2,
        )
        for zl in range(2)
        for g in range(4)
    ]


def call(kernel, shape, specs, out_spec=VMEM, scratch=()):
    make = lambda s: jax.ShapeDtypeStruct(s, jnp.bfloat16)
    many = isinstance(shape, list)
    return pl.pallas_call(
        kernel,
        out_shape=[make(s) for s in shape] if many else make(shape),
        in_specs=specs,
        out_specs=[out_spec] * len(shape) if many else out_spec,
        scratch_shapes=list(scratch),
        compiler_params=PARAMS,
    )


def in_hbm(a):
    return pltpu.with_memory_space_constraint(a, pltpu.HBM)


def swap_cores(a):
    return lax.ppermute(a, "core", [(0, 1), (1, 0)])


def body(built, build_order, p_pattern, q_pattern):
    parts = call(
        pick_kernel,
        (CHIPS, 12, PART, BS),
        [HBM, HBM],
        scratch=[
            pltpu.SMEM((64,), jnp.int32),
            pltpu.VMEM((4, CHIPS, PART, 8 * BS), jnp.bfloat16),
            pltpu.SemaphoreType.DMA((2,)),
        ],
    )(in_hbm(build_order), in_hbm(built.reshape(4, CHIPS, PART, 8 * BS)))
    parts = lax.all_to_all(parts, ("x", "zl"), 0, 0, tiled=True)
    placed = call(
        place_kernel,
        (24, PART, BS),
        [SMEM, SMEM, VMEM, VMEM],
        scratch=[pltpu.SMEM((64,), jnp.int32)],
    )(build_order, p_pattern, parts, swap_cores(parts))
    left = lax.ppermute(placed[19:], ("zl", "yl", "zh"), to_group(1))
    right = lax.ppermute(placed[:5], ("zl", "yl", "zh"), to_group(3))
    windows = call(
        window_kernel,
        (2 * CHIPS, WIN, PART, BS),
        [VMEM] * 3,
        scratch=[pltpu.VMEM((WIDE, PART, BS), jnp.bfloat16)],
    )(left, placed, right)
    windows = lax.all_to_all(windows, ("x", "zl", "yh"), 0, 0, tiled=True)
    return call(
        purify_kernel,
        (4 * BS, 8 * BS),
        [SMEM, VMEM, VMEM],
        scratch=[
            pltpu.VMEM((4, 5, BS, BS), jnp.float32),
            pltpu.VMEM((4, 5, BS, 2 * BS), jnp.bfloat16),
        ],
    )(q_pattern, windows, swap_cores(windows))


def solution(mesh):
    fine = Mesh(mesh.devices.reshape(GRID), AXES)
    placed = (P(ROW, COL), P(), P(), P())
    return jax.shard_map(
        body, mesh=fine, in_specs=placed, out_specs=P(ROW, COL), check_vma=False
    )
```

```python
import functools

import jax
import jax.numpy as jnp
import numpy as np
from jax import lax
from jax.experimental import pallas as pl
from jax.experimental.pallas import tpu as pltpu
from jax.sharding import Mesh
from jax.sharding import PartitionSpec as P

BS = 128
GRID = (4, 2, 2, 2, 2, 2)
AXES = ("x", "zl", "core", "yh", "yl", "zh")
ROW = ("x", "zl", "core")
COL = ("yh", "yl", "zh")
CHIPS = 8
PART = BS // CHIPS
PARTS = CHIPS * 12
WIDE = 34
WIN = 28
STARTS = (3, 6, 3, 0)

VMEM = pl.BlockSpec(memory_space=pltpu.VMEM)
SMEM = pl.BlockSpec(memory_space=pltpu.SMEM)
ANY = pl.BlockSpec(memory_space=pl.ANY)
HBM = pl.BlockSpec(memory_space=pltpu.HBM)
PARAMS = pltpu.CompilerParams(vmem_limit_bytes=48 * 1024 * 1024)


def chip_index():
    return lax.axis_index("x") * 2 + lax.axis_index("zl")


def group_index():
    return lax.axis_index("yl") * 2 + lax.axis_index("zh")


def pick_kernel(order, built, out, order_s, built_v, sem):
    copies = [
        pltpu.make_async_copy(order, order_s, sem.at[0]),
        pltpu.make_async_copy(built, built_v, sem.at[1]),
    ]
    for copy in copies:
        copy.start()
    for copy in copies:
        copy.wait()
    first = (chip_index() * 2 + lax.axis_index("core")) * 4
    zh = lax.axis_index("zh")
    for k in range(4):
        row = order_s[first + k]
        for d in range(3):
            col = lax.rem(row + d + 31, 8)
            at = pl.ds(pl.multiple_of(col * BS, BS), BS)
            for chip in range(0, CHIPS, 2):
                out[chip, 3 * k + d] = built_v[k, chip + zh, :, at]
                out[chip + 1, 3 * k + d] = built_v[k, chip + 1 - zh, :, at]


def find_kernel(order_in, pattern_in, ready, out, order, pattern, inverse, sem):
    core = lax.axis_index("core")
    yh = lax.axis_index("yh")
    base = group_index() * 8
    copies = [pltpu.make_async_copy(order_in, order, sem.at[0])]
    for n in range(3):
        rows = lax.rem(base + 8 * n + 24, 32) + 32 * core
        copies.append(
            pltpu.make_async_copy(
                pattern_in.at[pl.ds(pl.multiple_of(rows, 8), 8)],
                pattern.at[pl.ds(8 * n, 8)],
                sem.at[1 + n],
            )
        )
    for copy in copies:
        copy.start()
    copies[0].wait()
    for k in range(64):
        inverse[order[k]] = k
    for copy in copies[1:]:
        copy.wait()
    for bl in range(8):
        for e in range(3):
            row = lax.rem(base + bl + e + 31, 32) + 32 * core
            at = inverse[row]
            device = at // 4
            slot = (device // 2) * 12 + lax.rem(at, 4) * 3 + (2 - e)
            slot = jnp.where(lax.rem(device, 2) == core, slot, slot + PARTS)
            keep = pattern[7 + bl + e, base + bl + 32 * yh] != 0
            out[3 * bl + e] = jnp.where(keep, slot, 2 * PARTS)


def take(found, mine, other, n):
    at = found[n]
    here = at < PARTS
    at_mine = jnp.where(here, at, 0)
    at_other = jnp.where(jnp.logical_and(at >= PARTS, at < 2 * PARTS), at - PARTS, 0)
    value = jnp.where(here, mine[at_mine], other[at_other])
    return jnp.where(at < 2 * PARTS, value, jnp.zeros_like(value))


def edge_kernel(found, mine, other, first, last):
    for n in range(5):
        first[n] = take(found, mine, other, n)
        last[n] = take(found, mine, other, 19 + n)


def inner_kernel(found, mine, other, out):
    for n in range(14):
        out[n] = take(found, mine, other, 5 + n)


def distance(chip):
    return lax.rem(chip - group_index() + 8, 4)


def window_kernel(left, first, inner, last, right, out, wide):
    at = 0
    for ref in (left, first, inner, last, right):
        wide[at : at + ref.shape[0]] = ref[...]
        at += ref.shape[0]
    for chip in range(CHIPS):
        away = distance(chip)
        start = jnp.where(away == 1, STARTS[1], jnp.where(away == 3, STARTS[3], STARTS[0]))
        value = wide[pl.ds(start, WIN)]
        for half in range(2):
            out[2 * chip + half] = value


def clear_kernel(pattern, ready, out, flags, zeros, sem):
    zeros[...] = jnp.zeros_like(zeros)
    copies = [
        pltpu.make_async_copy(zeros, out.at[pl.ds(k * BS, BS)], sem.at[k]) for k in range(4)
    ]
    for copy in copies:
        copy.start()
    row_half = chip_index() // 4
    base = group_index() * 8
    for row in range(-2, 10):
        for col in range(max(-2, row - 2), min(9, row + 2) + 1):
            for half in range(2):
                i = lax.rem(base + row + 32, 32) + 32 * row_half
                j = lax.rem(base + col + 32, 32) + 32 * half
                flags[row + 2, 2 * (col + 2) + half] = pattern[i, j]
    for copy in copies:
        copy.wait()


def purify_kernel(flags_in, mine, other, cleared, out, flags, squares, rounded, result, sem):
    fetch = pltpu.make_async_copy(flags_in, flags, sem.at[4])
    fetch.start()
    core = lax.axis_index("core")
    yh = lax.axis_index("yh")
    zh = lax.axis_index("zh")
    chip = chip_index()
    away = distance(chip)
    row_half = chip // 4

    def dot(a, b):
        return jnp.dot(a, b, preferred_element_type=jnp.float32)

    def block(ref, n, half):
        rows = [ref[2 * (p + zh if p % 2 == 0 else p - zh) + half, n] for p in range(CHIPS)]
        return jnp.concatenate(rows, 0)

    def kept(row, col, half):
        return flags[row + 2, 2 * (col + 2) + half] != 0

    def work(u, start, rows, results):
        halves = (mine, other) if u == 0 else (other, mine)
        same = row_half == u

        def number(row, col):
            return 2 * col + row + 6 - start

        def column(row, col, half):
            return jnp.concatenate([block(h, number(row, col), half) for h in halves], 0)

        def whole(row, col):
            return jnp.concatenate([column(row, col, half) for half in range(2)], 1)

        def left(row, col):
            n = number(row, col)
            parts = [
                jnp.where(same, block(mine, n, half), block(other, n, half)) for half in range(2)
            ]
            return jnp.concatenate(parts, 1)

        near = lambda a, b, d=1: abs(a - b) <= d
        span = range(-2, 10)
        cols = {a: sorted({k for b, j in results if b == a for k in span if near(k, j) and near(k, a, 2)}) for a in rows}
        copies = []
        for r_at, a in enumerate(rows):
            first = cols[a][0]
            for k in cols[a]:
                ls = [l for l in span if near(l, a) and near(l, k)]
                total = dot(
                    jnp.concatenate([left(a, l) for l in ls], 1),
                    jnp.concatenate([whole(l, k) for l in ls], 0),
                )
                if r_at == 0 and k == first:
                    fetch.wait()
                parts = []
                for half in range(2):
                    part = total[:, half * BS : (half + 1) * BS]
                    parts.append(jnp.where(kept(a, k, half), part, jnp.zeros_like(part)))
                squares[r_at, k - first] = jnp.where(yh == 0, parts[0], parts[1])
                rounded[r_at, k - first] = jnp.concatenate(parts, 1).astype(jnp.bfloat16)
            spots = [(j, r, c) for (b, j), (r, c) in results.items() if b == a]
            for j, r, c in spots:
                ks = [k for k in cols[a] if near(k, j)]
                total = dot(
                    jnp.concatenate([rounded[r_at, k - first] for k in ks], 1),
                    jnp.concatenate([column(k, j, yh) for k in ks], 0),
                )
                value = 3.0 * squares[r_at, j - first] - 2.0 * total
                value = jnp.where(kept(a, j, yh), value, jnp.zeros_like(value))
                result[r, :, c * BS : (c + 1) * BS] = value.astype(jnp.bfloat16)
            r = spots[0][1]
            low, high = min(c for *_, c in spots) * BS, (max(c for *_, c in spots) + 1) * BS
            copies.append(
                pltpu.make_async_copy(
                    result.at[r, :, low:high],
                    out.at[pl.ds(r * BS, BS), low:high],
                    sem.at[r_at],
                )
            )
            copies[-1].start()
        for copy in copies:
            copy.wait()

    for u in range(2):

        @pl.when(jnp.logical_and(away == 0, core == u))
        def _(u=u):
            rows = list(range(4 * u, 4 * u + 4))
            spots = [(a, j) for a in rows for j in range(a - 2, a + 3) if 0 <= j < 8]
            work(u, STARTS[0], rows, {(a, j): (a - 4 * u, j) for a, j in spots})

    @pl.when(jnp.logical_and(away == 1, core == 0))
    def _():
        work(0, STARTS[1], [8, 9], {(8, 6): (0, 6), (8, 7): (0, 7), (9, 7): (1, 7)})

    last = jnp.logical_and(away == 3, core == 1)
    near_one = jnp.logical_or(jnp.logical_and(away == 1, core == 0), last)

    @pl.when(jnp.logical_and(away != 0, jnp.logical_not(near_one)))
    def _():
        fetch.wait()

    @pl.when(last)
    def _():
        work(1, STARTS[3], [-1, -2], {(-1, 1): (3, 1), (-1, 0): (3, 0), (-2, 0): (2, 0)})


def to_group(step):
    return [
        (
            ((zl * 2 + g // 2) * 2) + g % 2,
            (((1 - zl) * 2 + (g + step) % 4 // 2) * 2) + (g + step) % 2,
        )
        for zl in range(2)
        for g in range(4)
    ]


def bf16(*shape):
    return jax.ShapeDtypeStruct(shape, jnp.bfloat16)


def call(kernel, out_shape, in_specs, out_specs=VMEM, scratch=(), **options):
    if isinstance(out_shape, list) and not isinstance(out_specs, list):
        out_specs = [out_specs] * len(out_shape)
    return pl.pallas_call(
        kernel,
        out_shape=out_shape,
        in_specs=in_specs,
        out_specs=out_specs,
        scratch_shapes=list(scratch),
        compiler_params=PARAMS,
        **options,
    )


def in_hbm(a):
    return pltpu.with_memory_space_constraint(a, pltpu.HBM)


def swap_cores(a):
    return lax.ppermute(a, "core", [(0, 1), (1, 0)])


def body(built, build_order, p_pattern, q_pattern):
    parts = call(
        pick_kernel,
        bf16(CHIPS, 12, PART, BS),
        [HBM, HBM],
        scratch=[
            pltpu.SMEM((64,), jnp.int32),
            pltpu.VMEM((4, CHIPS, PART, 8 * BS), jnp.bfloat16),
            pltpu.SemaphoreType.DMA((2,)),
        ],
    )(in_hbm(build_order), in_hbm(built.reshape(4, CHIPS, PART, 8 * BS)))
    parts = lax.all_to_all(parts, ("x", "zl"), 0, 0, tiled=True).reshape(PARTS, PART, BS)
    found = call(
        find_kernel,
        jax.ShapeDtypeStruct((24,), jnp.int32),
        [ANY, ANY, ANY],
        SMEM,
        [
            pltpu.SMEM((64,), jnp.int32),
            pltpu.SMEM((24, 64), jnp.int32),
            pltpu.SMEM((64,), jnp.int32),
            pltpu.SemaphoreType.DMA((4,)),
        ],
    )(build_order, p_pattern, parts)
    both = (parts, swap_cores(parts))
    edges = [SMEM, VMEM, VMEM]
    first, last = call(edge_kernel, [bf16(5, PART, BS)] * 2, edges)(found, *both)
    left = lax.ppermute(last, ("zl", "yl", "zh"), to_group(1))
    right = lax.ppermute(first, ("zl", "yl", "zh"), to_group(3))
    inner = call(inner_kernel, bf16(14, PART, BS), edges)(found, *both)
    windows = call(
        window_kernel,
        bf16(2 * CHIPS, WIN, PART, BS),
        [VMEM] * 5,
        scratch=[pltpu.VMEM((WIDE, PART, BS), jnp.bfloat16)],
    )(left, first, inner, last, right)
    windows = lax.all_to_all(windows, ("x", "zl", "yh"), 0, 0, tiled=True)
    cleared, flags = call(
        clear_kernel,
        [pltpu.HBM((4 * BS, 8 * BS), jnp.bfloat16), jax.ShapeDtypeStruct((12, 24), jnp.int32)],
        [SMEM, ANY],
        [HBM, SMEM],
        [pltpu.VMEM((BS, 8 * BS), jnp.bfloat16), pltpu.SemaphoreType.DMA((4,))],
    )(q_pattern, windows)
    return call(
        purify_kernel,
        bf16(4 * BS, 8 * BS),
        [ANY, VMEM, VMEM, HBM],
        HBM,
        [
            pltpu.SMEM((12, 24), jnp.int32),
            pltpu.VMEM((4, 5, BS, BS), jnp.float32),
            pltpu.VMEM((4, 5, BS, 2 * BS), jnp.bfloat16),
            pltpu.VMEM((4, BS, 8 * BS), jnp.bfloat16),
            pltpu.SemaphoreType.DMA((5,)),
        ],
        input_output_aliases={3: 0},
    )(flags, windows, swap_cores(windows), cleared)


def solution(mesh):
    fine = Mesh(mesh.devices.reshape(GRID), AXES)
    placed = (P(ROW, COL), P(), P(), P())
    return jax.shard_map(
        body, mesh=fine, in_specs=placed, out_specs=P(ROW, COL), check_vma=False
    )
```

```python
import functools

import jax
import jax.numpy as jnp
import numpy as np
from jax import lax
from jax.experimental import pallas as pl
from jax.experimental.pallas import tpu as pltpu
from jax.sharding import Mesh
from jax.sharding import PartitionSpec as P

BS = 128
GRID = (4, 2, 2, 2, 2, 2)
AXES = ("x", "zl", "core", "yh", "yl", "zh")
ROW = ("x", "zl", "core")
COL = ("yh", "yl", "zh")
CHIPS = 8
PART = BS // CHIPS
PARTS = CHIPS * 12
WIDE = 34
WIN = 28
SHARED = 18

VMEM = pl.BlockSpec(memory_space=pltpu.VMEM)
SMEM = pl.BlockSpec(memory_space=pltpu.SMEM)
ANY = pl.BlockSpec(memory_space=pl.ANY)
HBM = pl.BlockSpec(memory_space=pltpu.HBM)
PARAMS = pltpu.CompilerParams(vmem_limit_bytes=48 * 1024 * 1024)


def chip_index():
    return lax.axis_index("x") * 2 + lax.axis_index("zl")


def group_index():
    return lax.axis_index("yl") * 2 + lax.axis_index("zh")


def pick_kernel(order, built, out, order_s, built_v, sem):
    copies = [
        pltpu.make_async_copy(order, order_s, sem.at[0]),
        pltpu.make_async_copy(built, built_v, sem.at[1]),
    ]
    for copy in copies:
        copy.start()
    for copy in copies:
        copy.wait()
    first = (chip_index() * 2 + lax.axis_index("core")) * 4
    zh = lax.axis_index("zh")
    for k in range(4):
        row = order_s[first + k]
        for d in range(3):
            col = lax.rem(row + d + 31, 8)
            at = pl.ds(pl.multiple_of(col * BS, BS), BS)
            for chip in range(0, CHIPS, 2):
                out[chip, 3 * k + d] = built_v[k, chip + zh, :, at]
                out[chip + 1, 3 * k + d] = built_v[k, chip + 1 - zh, :, at]


def search(order_in, pattern_in, order, pattern, inverse, sem):
    core = lax.axis_index("core")
    yh = lax.axis_index("yh")
    base = group_index() * 8
    copies = [pltpu.make_async_copy(order_in, order, sem.at[0])]
    for half in range(2):
        for n in range(3):
            rows = lax.rem(base + 8 * n + 24, 32) + 32 * half
            to = 3 * half + n
            copies.append(
                pltpu.make_async_copy(
                    pattern_in.at[pl.ds(pl.multiple_of(rows, 8), 8)],
                    pattern.at[pl.ds(8 * to, 8)],
                    sem.at[1 + to],
                )
            )
    for copy in copies:
        copy.start()
    copies[0].wait()
    for k in range(64):
        inverse[order[k]] = k
    for copy in copies[1:]:
        copy.wait()

    def find(half, n):
        bl, e = (n // 3, n % 3) if isinstance(n, int) else (lax.div(n, 3), lax.rem(n, 3))
        at = inverse[lax.rem(base + bl + e + 31, 32) + 32 * half]
        device = at // 4
        slot = (device // 2) * 12 + lax.rem(at, 4) * 3 + (2 - e)
        slot = jnp.where(lax.rem(device, 2) == core, slot, slot + PARTS)
        keep = pattern[24 * half + 7 + bl + e, base + bl + 32 * yh] != 0
        return jnp.where(keep, slot, 2 * PARTS)

    return find


SEARCH = [
    pltpu.SMEM((64,), jnp.int32),
    pltpu.SMEM((48, 64), jnp.int32),
    pltpu.SMEM((64,), jnp.int32),
    pltpu.SemaphoreType.DMA((7,)),
]


def edge_find_kernel(order_in, pattern_in, ready, out, *scratch):
    find = search(order_in, pattern_in, *scratch)
    first = 19 * (1 - lax.axis_index("core"))
    for half in range(2):
        for n in range(5):
            out[5 * half + n] = find(half, first + n)


def take(at, mine, other):
    here = at < PARTS
    at_mine = jnp.where(here, at, 0)
    at_other = jnp.where(jnp.logical_and(at >= PARTS, at < 2 * PARTS), at - PARTS, 0)
    value = jnp.where(here, mine[at_mine], other[at_other])
    return jnp.where(at < 2 * PARTS, value, jnp.zeros_like(value))


def edge_kernel(found, mine, other, out):
    for n in range(10):
        out[n] = take(found[n], mine, other)


def own_kernel(order_in, pattern_in, mine, other, edge, out, *scratch):
    find = search(order_in, pattern_in, *scratch)
    for half in range(2):
        for n in range(24):
            out[24 * half + n] = take(find(half, n), mine, other)


def flags_kernel(pattern_in, ready, flags, pattern, sem):
    base = group_index() * 8
    copies = []
    for n in range(3):
        rows = lax.rem(base + 8 * n + 24, 32) + 32 * (chip_index() // 4)
        copies.append(
            pltpu.make_async_copy(
                pattern_in.at[pl.ds(pl.multiple_of(rows, 8), 8)],
                pattern.at[pl.ds(8 * n, 8)],
                sem.at[n],
            )
        )
        copies[-1].start()
    for copy in copies:
        copy.wait()
    for row in range(-2, 10):
        for col in range(max(-2, row - 2), min(9, row + 2) + 1):
            j = lax.rem(base + col + 32, 32)
            for half in range(2):
                flags[row + 2, 2 * (col + 2) + half] = pattern[8 + row, j + 32 * half]


def distance(chip):
    return lax.rem(chip - group_index() + 8, 4)


def window_kernel(beside, own, ready, out, wide):
    for half in range(2):
        wide[half, 0:5] = beside[5 * half : 5 * half + 5]
        wide[half, 5:29] = own[24 * half : 24 * half + 24]
        wide[half, 29:34] = beside[5 * half : 5 * half + 5]
    core = lax.axis_index("core")
    for chip in range(CHIPS):
        away = distance(chip)
        right, left = away == 1, away == 3
        edge = jnp.logical_or(right, left)
        pick = lambda r, l, other: jnp.where(right, r, jnp.where(left, l, other))
        alone = pick(24, 5, 3 + 19 * core)
        for half in range(2):
            at = 2 * chip + half
            for h in range(2):
                out[at, 9 * h : 9 * h + 9] = wide[h, pl.ds(alone, 9)]
                shared = wide[jnp.where(edge, h, core), pl.ds(pick(29, 0, 12 + 5 * h), 5)]
                out[at, SHARED + 5 * h : SHARED + 5 * h + 5] = shared


def clear_kernel(ready, out, zeros, sem):
    zeros[...] = jnp.zeros_like(zeros)
    copies = [
        pltpu.make_async_copy(zeros, out.at[pl.ds(k * BS, BS)], sem.at[k]) for k in range(4)
    ]
    for copy in copies:
        copy.start()
    for copy in copies:
        copy.wait()


def purify_kernel(flags_in, mine, other, cleared, out, flags, squares, rounded, result, sem):
    fetch = pltpu.make_async_copy(flags_in, flags, sem.at[4])
    fetch.start()
    core = lax.axis_index("core")
    yh = lax.axis_index("yh")
    zh = lax.axis_index("zh")
    chip = chip_index()
    away = distance(chip)
    row_half = chip // 4

    def dot(a, b):
        return jnp.dot(a, b, preferred_element_type=jnp.float32)

    def block(ref, n, half):
        rows = [ref[2 * (p + zh if p % 2 == 0 else p - zh) + half, n] for p in range(CHIPS)]
        return jnp.concatenate(rows, 0)

    def kept(row, col, half):
        return flags[row + 2, 2 * (col + 2) + half] != 0

    def work(locate, rows, results):
        def half_block(f, h, half):
            n = locate(f, h)
            return block(mine, n, half) if n >= 0 else block(other, n + 10, half)

        def number(row, col):
            return 2 * col + row + 6

        def column(row, col, half):
            return jnp.concatenate([half_block(number(row, col), h, half) for h in range(2)], 0)

        def whole(row, col):
            return jnp.concatenate([column(row, col, half) for half in range(2)], 1)

        def left(row, col):
            f = number(row, col)
            low, high = locate(f, 0), locate(f, 1)
            if low >= 0 and high >= 0:
                n = low + row_half * (high - low)
                return jnp.concatenate([block(mine, n, half) for half in range(2)], 1)
            parts = [
                jnp.where(row_half == 0, half_block(f, 0, half), half_block(f, 1, half))
                for half in range(2)
            ]
            return jnp.concatenate(parts, 1)

        near = lambda a, b, d=1: abs(a - b) <= d
        span = range(-2, 10)
        cols = {a: sorted({k for b, j in results if b == a for k in span if near(k, j) and near(k, a, 2)}) for a in rows}
        copies = []
        for r_at, a in enumerate(rows):
            first = cols[a][0]
            for k in cols[a]:
                ls = [l for l in span if near(l, a) and near(l, k)]
                total = dot(
                    jnp.concatenate([left(a, l) for l in ls], 1),
                    jnp.concatenate([whole(l, k) for l in ls], 0),
                )
                if r_at == 0 and k == first:
                    fetch.wait()
                parts = []
                for half in range(2):
                    part = total[:, half * BS : (half + 1) * BS]
                    parts.append(jnp.where(kept(a, k, half), part, jnp.zeros_like(part)))
                squares[r_at, k - first] = jnp.where(yh == 0, parts[0], parts[1])
                rounded[r_at, k - first] = jnp.concatenate(parts, 1).astype(jnp.bfloat16)
            spots = [(j, r, c) for (b, j), (r, c) in results.items() if b == a]
            for j, r, c in spots:
                ks = [k for k in cols[a] if near(k, j)]
                total = dot(
                    jnp.concatenate([rounded[r_at, k - first] for k in ks], 1),
                    jnp.concatenate([column(k, j, yh) for k in ks], 0),
                )
                value = 3.0 * squares[r_at, j - first] - 2.0 * total
                value = jnp.where(kept(a, j, yh), value, jnp.zeros_like(value))
                result[r, :, c * BS : (c + 1) * BS] = value.astype(jnp.bfloat16)
            r = spots[0][1]
            low, high = min(c for *_, c in spots) * BS, (max(c for *_, c in spots) + 1) * BS
            copies.append(
                pltpu.make_async_copy(
                    result.at[r, :, low:high],
                    out.at[pl.ds(r * BS, BS), low:high],
                    sem.at[r_at],
                )
            )
            copies[-1].start()
        for copy in copies:
            copy.wait()

    def low(f, h):
        return f - 3 + 9 * h if f < 12 else SHARED + f - 12 if h == 0 else f - 22

    def high(f, h):
        return f - 22 + 9 * h if f > 21 else SHARED + f - 12 if h == 1 else f - 22

    def beyond(f, h):
        return f - 24 + 9 * h if f < 29 else f - 39 + 5 * h

    def before(f, h):
        return f - 5 + 9 * h if f > 4 else f - 10 + 5 * h

    for u, locate in enumerate((low, high)):

        @pl.when(jnp.logical_and(away == 0, core == u))
        def _(u=u, locate=locate):
            rows = list(range(4 * u, 4 * u + 4))
            spots = [(a, j) for a in rows for j in range(a - 2, a + 3) if 0 <= j < 8]
            work(locate, rows, {(a, j): (a - 4 * u, j) for a, j in spots})

    @pl.when(jnp.logical_and(away == 1, core == 0))
    def _():
        work(beyond, [8, 9], {(8, 6): (0, 6), (8, 7): (0, 7), (9, 7): (1, 7)})

    last = jnp.logical_and(away == 3, core == 1)
    near_one = jnp.logical_or(jnp.logical_and(away == 1, core == 0), last)

    @pl.when(jnp.logical_and(away != 0, jnp.logical_not(near_one)))
    def _():
        fetch.wait()

    @pl.when(last)
    def _():
        work(before, [-1, -2], {(-1, 1): (3, 1), (-1, 0): (3, 0), (-2, 0): (2, 0)})


def to_groups():
    index = lambda zl, core, g: (zl * 2 + core) * 4 + g % 4
    return [
        (index(zl, core, g), index(1 - zl, core, g + (3 if core else 1)))
        for zl in range(2)
        for core in range(2)
        for g in range(4)
    ]


def bf16(*shape):
    return jax.ShapeDtypeStruct(shape, jnp.bfloat16)


def call(kernel, out_shape, in_specs, out_specs=VMEM, scratch=(), **options):
    if isinstance(out_shape, list) and not isinstance(out_specs, list):
        out_specs = [out_specs] * len(out_shape)
    return pl.pallas_call(
        kernel,
        out_shape=out_shape,
        in_specs=in_specs,
        out_specs=out_specs,
        scratch_shapes=list(scratch),
        compiler_params=PARAMS,
        **options,
    )


def in_hbm(a):
    return pltpu.with_memory_space_constraint(a, pltpu.HBM)


def swap_cores(a):
    return lax.ppermute(a, "core", [(0, 1), (1, 0)])


def body(built, build_order, p_pattern, q_pattern):
    parts = call(
        pick_kernel,
        bf16(CHIPS, 12, PART, BS),
        [HBM, HBM],
        scratch=[
            pltpu.SMEM((64,), jnp.int32),
            pltpu.VMEM((4, CHIPS, PART, 8 * BS), jnp.bfloat16),
            pltpu.SemaphoreType.DMA((2,)),
        ],
    )(in_hbm(build_order), in_hbm(built.reshape(4, CHIPS, PART, 8 * BS)))
    parts = lax.all_to_all(parts, ("x", "zl"), 0, 0, tiled=True).reshape(PARTS, PART, BS)
    found = call(
        edge_find_kernel, jax.ShapeDtypeStruct((10,), jnp.int32), [ANY] * 3, SMEM, SEARCH
    )(build_order, p_pattern, parts)
    both = (parts, swap_cores(parts))
    edge = call(edge_kernel, bf16(10, PART, BS), [SMEM, VMEM, VMEM])(found, *both)
    beside = lax.ppermute(edge, ("zl", "core", "yl", "zh"), to_groups())
    own = call(
        own_kernel, bf16(48, PART, BS), [ANY, ANY, VMEM, VMEM, ANY], scratch=SEARCH
    )(build_order, p_pattern, *both, edge)
    cleared = call(
        clear_kernel,
        pltpu.HBM((4 * BS, 8 * BS), jnp.bfloat16),
        [ANY],
        HBM,
        [pltpu.VMEM((BS, 8 * BS), jnp.bfloat16), pltpu.SemaphoreType.DMA((4,))],
    )(edge)
    windows = call(
        window_kernel,
        bf16(2 * CHIPS, WIN, PART, BS),
        [VMEM, VMEM, HBM],
        scratch=[pltpu.VMEM((2, WIDE, PART, BS), jnp.bfloat16)],
    )(beside, own, in_hbm(cleared))
    windows = lax.all_to_all(windows, ("x", "zl", "yh"), 0, 0, tiled=True)
    flags = call(
        flags_kernel,
        jax.ShapeDtypeStruct((12, 24), jnp.int32),
        [ANY, ANY],
        SMEM,
        [pltpu.SMEM((24, 64), jnp.int32), pltpu.SemaphoreType.DMA((3,))],
    )(q_pattern, windows)
    return call(
        purify_kernel,
        bf16(4 * BS, 8 * BS),
        [ANY, VMEM, VMEM, HBM],
        HBM,
        [
            pltpu.SMEM((12, 24), jnp.int32),
            pltpu.VMEM((4, 5, BS, BS), jnp.float32),
            pltpu.VMEM((4, 5, BS, 2 * BS), jnp.bfloat16),
            pltpu.VMEM((4, BS, 8 * BS), jnp.bfloat16),
            pltpu.SemaphoreType.DMA((5,)),
        ],
        input_output_aliases={3: 0},
    )(flags, windows, swap_cores(windows[:, SHARED:]), cleared)


def solution(mesh):
    fine = Mesh(mesh.devices.reshape(GRID), AXES)
    placed = (P(ROW, COL), P(), P(), P())
    return jax.shard_map(
        body, mesh=fine, in_specs=placed, out_specs=P(ROW, COL), check_vma=False
    )
```

```python
import functools

import jax
import jax.numpy as jnp
import numpy as np
from jax import lax
from jax.experimental import pallas as pl
from jax.experimental.pallas import tpu as pltpu
from jax.sharding import Mesh
from jax.sharding import PartitionSpec as P

BS = 128
GRID = (4, 2, 2, 2, 2, 2)
AXES = ("x", "zl", "core", "yh", "yl", "zh")
ROW = ("x", "zl", "core")
COL = ("yh", "yl", "zh")
CHIPS = 8
PART = BS // CHIPS
PARTS = CHIPS * 12
WIDE = 34
WIN = 28
SHARED = 18

VMEM = pl.BlockSpec(memory_space=pltpu.VMEM)
SMEM = pl.BlockSpec(memory_space=pltpu.SMEM)
ANY = pl.BlockSpec(memory_space=pl.ANY)
HBM = pl.BlockSpec(memory_space=pltpu.HBM)
PARAMS = pltpu.CompilerParams(vmem_limit_bytes=48 * 1024 * 1024)


def chip_index():
    return lax.axis_index("x") * 2 + lax.axis_index("zl")


def group_index():
    return lax.axis_index("yl") * 2 + lax.axis_index("zh")


def pick_kernel(order, built, out, order_s, built_v, sem):
    fetch = pltpu.make_async_copy(order, order_s, sem.at[4])
    fetch.start()
    copies = [pltpu.make_async_copy(built.at[k], built_v.at[k], sem.at[k]) for k in range(4)]
    for copy in copies:
        copy.start()
    fetch.wait()
    first = (chip_index() * 2 + lax.axis_index("core")) * 4
    zh = lax.axis_index("zh")
    for k in range(4):
        row = order_s[first + k]
        copies[k].wait()
        for d in range(3):
            col = lax.rem(row + d + 31, 8)
            at = pl.ds(pl.multiple_of(col * BS, BS), BS)
            for chip in range(0, CHIPS, 2):
                out[chip, 3 * k + d] = built_v[k, chip + zh, :, at]
                out[chip + 1, 3 * k + d] = built_v[k, chip + 1 - zh, :, at]


def search(order_in, pattern_in, order, pattern, inverse, sem):
    core = lax.axis_index("core")
    yh = lax.axis_index("yh")
    base = group_index() * 8
    copies = [pltpu.make_async_copy(order_in, order, sem.at[0])]
    for half in range(2):
        for n in range(3):
            rows = lax.rem(base + 8 * n + 24, 32) + 32 * half
            to = 3 * half + n
            copies.append(
                pltpu.make_async_copy(
                    pattern_in.at[pl.ds(pl.multiple_of(rows, 8), 8)],
                    pattern.at[pl.ds(8 * to, 8)],
                    sem.at[1 + to],
                )
            )
    for copy in copies:
        copy.start()
    copies[0].wait()
    for k in range(64):
        inverse[order[k]] = k
    for copy in copies[1:]:
        copy.wait()

    def find(half, n):
        bl, e = (n // 3, n % 3) if isinstance(n, int) else (lax.div(n, 3), lax.rem(n, 3))
        at = inverse[lax.rem(base + bl + e + 31, 32) + 32 * half]
        device = at // 4
        slot = (device // 2) * 12 + lax.rem(at, 4) * 3 + (2 - e)
        slot = jnp.where(lax.rem(device, 2) == core, slot, slot + PARTS)
        keep = pattern[24 * half + 7 + bl + e, base + bl + 32 * yh] != 0
        return jnp.where(keep, slot, 2 * PARTS)

    return find


SEARCH = [
    pltpu.SMEM((64,), jnp.int32),
    pltpu.SMEM((48, 64), jnp.int32),
    pltpu.SMEM((64,), jnp.int32),
    pltpu.SemaphoreType.DMA((7,)),
]


def edge_find_kernel(order_in, pattern_in, ready, out, *scratch):
    find = search(order_in, pattern_in, *scratch)
    first = 19 * (1 - lax.axis_index("core"))
    for half in range(2):
        for n in range(5):
            out[5 * half + n] = find(half, first + n)


def take(at, mine, other):
    here = at < PARTS
    at_mine = jnp.where(here, at, 0)
    at_other = jnp.where(jnp.logical_and(at >= PARTS, at < 2 * PARTS), at - PARTS, 0)
    value = jnp.where(here, mine[at_mine], other[at_other])
    return jnp.where(at < 2 * PARTS, value, jnp.zeros_like(value))


def edge_kernel(found, mine, other, out):
    for n in range(10):
        out[n] = take(found[n], mine, other)


def own_kernel(order_in, pattern_in, mine, other, edge, out, *scratch):
    find = search(order_in, pattern_in, *scratch)
    for half in range(2):
        for n in range(24):
            out[24 * half + n] = take(find(half, n), mine, other)


def flags_kernel(pattern_in, ready, flags, pattern, sem):
    base = group_index() * 8
    copies = []
    for n in range(3):
        rows = lax.rem(base + 8 * n + 24, 32) + 32 * (chip_index() // 4)
        copies.append(
            pltpu.make_async_copy(
                pattern_in.at[pl.ds(pl.multiple_of(rows, 8), 8)],
                pattern.at[pl.ds(8 * n, 8)],
                sem.at[n],
            )
        )
        copies[-1].start()
    for copy in copies:
        copy.wait()
    for row in range(-2, 10):
        for col in range(max(-2, row - 2), min(9, row + 2) + 1):
            j = lax.rem(base + col + 32, 32)
            for half in range(2):
                flags[row + 2, 2 * (col + 2) + half] = pattern[8 + row, j + 32 * half]


def distance(chip):
    return lax.rem(chip - group_index() + 8, 4)


def window_kernel(beside, own, ready, out, wide):
    for half in range(2):
        wide[half, 0:5] = beside[5 * half : 5 * half + 5]
        wide[half, 5:29] = own[24 * half : 24 * half + 24]
        wide[half, 29:34] = beside[5 * half : 5 * half + 5]
    core = lax.axis_index("core")
    for chip in range(CHIPS):
        away = distance(chip)
        right, left = away == 1, away == 3
        edge = jnp.logical_or(right, left)
        pick = lambda r, l, other: jnp.where(right, r, jnp.where(left, l, other))
        alone = pick(24, 5, 3 + 19 * core)
        for half in range(2):
            at = 2 * chip + half
            for h in range(2):
                out[at, 9 * h : 9 * h + 9] = wide[h, pl.ds(alone, 9)]
                shared = wide[jnp.where(edge, h, core), pl.ds(pick(29, 0, 12 + 5 * h), 5)]
                out[at, SHARED + 5 * h : SHARED + 5 * h + 5] = shared


def clear_kernel(ready, out, zeros, sem):
    zeros[...] = jnp.zeros_like(zeros)
    copies = [
        pltpu.make_async_copy(zeros, out.at[pl.ds(k * BS, BS)], sem.at[k]) for k in range(4)
    ]
    for copy in copies:
        copy.start()
    for copy in copies:
        copy.wait()


def purify_kernel(flags_in, mine, other, cleared, out, flags, squares, rounded, result, sem):
    fetch = pltpu.make_async_copy(flags_in, flags, sem.at[4])
    fetch.start()
    core = lax.axis_index("core")
    yh = lax.axis_index("yh")
    zh = lax.axis_index("zh")
    chip = chip_index()
    away = distance(chip)
    row_half = chip // 4

    def dot(a, b):
        return jnp.dot(a, b, preferred_element_type=jnp.float32)

    def block(ref, n, half):
        rows = [ref[2 * (p + zh if p % 2 == 0 else p - zh) + half, n] for p in range(CHIPS)]
        return jnp.concatenate(rows, 0)

    def kept(row, col, half):
        return flags[row + 2, 2 * (col + 2) + half] != 0

    def work(locate, rows, results):
        def half_block(f, h, half):
            n = locate(f, h)
            return block(mine, n, half) if n >= 0 else block(other, n + 10, half)

        def number(row, col):
            return 2 * col + row + 6

        def column(row, col, half):
            return jnp.concatenate([half_block(number(row, col), h, half) for h in range(2)], 0)

        def whole(row, col):
            return jnp.concatenate([column(row, col, half) for half in range(2)], 1)

        def left(row, col):
            f = number(row, col)
            low, high = locate(f, 0), locate(f, 1)
            if low >= 0 and high >= 0:
                n = low + row_half * (high - low)
                return jnp.concatenate([block(mine, n, half) for half in range(2)], 1)
            parts = [
                jnp.where(row_half == 0, half_block(f, 0, half), half_block(f, 1, half))
                for half in range(2)
            ]
            return jnp.concatenate(parts, 1)

        near = lambda a, b, d=1: abs(a - b) <= d
        span = range(-2, 10)
        cols = {a: sorted({k for b, j in results if b == a for k in span if near(k, j) and near(k, a, 2)}) for a in rows}
        copies = []
        for r_at, a in enumerate(rows):
            first = cols[a][0]
            for k in cols[a]:
                ls = [l for l in span if near(l, a) and near(l, k)]
                total = dot(
                    jnp.concatenate([left(a, l) for l in ls], 1),
                    jnp.concatenate([whole(l, k) for l in ls], 0),
                )
                if r_at == 0 and k == first:
                    fetch.wait()
                parts = []
                for half in range(2):
                    part = total[:, half * BS : (half + 1) * BS]
                    parts.append(jnp.where(kept(a, k, half), part, jnp.zeros_like(part)))
                squares[r_at, k - first] = jnp.where(yh == 0, parts[0], parts[1])
                rounded[r_at, k - first] = jnp.concatenate(parts, 1).astype(jnp.bfloat16)
            spots = [(j, r, c) for (b, j), (r, c) in results.items() if b == a]
            js = [j for j, _, _ in spots]
            totals = {}
            for pair in [js[n : n + 2] for n in range(0, len(js), 2)]:
                ks = [k for k in cols[a] if any(near(k, j) for j in pair)]
                rights = [
                    [column(k, j, yh) if near(k, j) else jnp.zeros((2 * BS, BS), jnp.bfloat16) for j in pair]
                    for k in ks
                ]
                total = dot(
                    jnp.concatenate([rounded[r_at, k - first] for k in ks], 1),
                    jnp.concatenate([jnp.concatenate(right, 1) for right in rights], 0),
                )
                for n, j in enumerate(pair):
                    totals[j] = total[:, n * BS : (n + 1) * BS]
            for j, r, c in spots:
                value = 3.0 * squares[r_at, j - first] - 2.0 * totals[j]
                value = jnp.where(kept(a, j, yh), value, jnp.zeros_like(value))
                result[r, :, c * BS : (c + 1) * BS] = value.astype(jnp.bfloat16)
            r = spots[0][1]
            low, high = min(c for *_, c in spots) * BS, (max(c for *_, c in spots) + 1) * BS
            copies.append(
                pltpu.make_async_copy(
                    result.at[r, :, low:high],
                    out.at[pl.ds(r * BS, BS), low:high],
                    sem.at[r_at],
                )
            )
            copies[-1].start()
        for copy in copies:
            copy.wait()

    def low(f, h):
        return f - 3 + 9 * h if f < 12 else SHARED + f - 12 if h == 0 else f - 22

    def high(f, h):
        return f - 22 + 9 * h if f > 21 else SHARED + f - 12 if h == 1 else f - 22

    def beyond(f, h):
        return f - 24 + 9 * h if f < 29 else f - 39 + 5 * h

    def before(f, h):
        return f - 5 + 9 * h if f > 4 else f - 10 + 5 * h

    for u, locate in enumerate((low, high)):

        @pl.when(jnp.logical_and(away == 0, core == u))
        def _(u=u, locate=locate):
            rows = list(range(4 * u, 4 * u + 4))
            spots = [(a, j) for a in rows for j in range(a - 2, a + 3) if 0 <= j < 8]
            work(locate, rows, {(a, j): (a - 4 * u, j) for a, j in spots})

    @pl.when(jnp.logical_and(away == 1, core == 0))
    def _():
        work(beyond, [8, 9], {(8, 6): (0, 6), (8, 7): (0, 7), (9, 7): (1, 7)})

    last = jnp.logical_and(away == 3, core == 1)
    near_one = jnp.logical_or(jnp.logical_and(away == 1, core == 0), last)

    @pl.when(jnp.logical_and(away != 0, jnp.logical_not(near_one)))
    def _():
        fetch.wait()

    @pl.when(last)
    def _():
        work(before, [-1, -2], {(-1, 1): (3, 1), (-1, 0): (3, 0), (-2, 0): (2, 0)})


def to_groups():
    index = lambda zl, core, g: (zl * 2 + core) * 4 + g % 4
    return [
        (index(zl, core, g), index(1 - zl, core, g + (3 if core else 1)))
        for zl in range(2)
        for core in range(2)
        for g in range(4)
    ]


def bf16(*shape):
    return jax.ShapeDtypeStruct(shape, jnp.bfloat16)


def call(kernel, out_shape, in_specs, out_specs=VMEM, scratch=(), **options):
    if isinstance(out_shape, list) and not isinstance(out_specs, list):
        out_specs = [out_specs] * len(out_shape)
    return pl.pallas_call(
        kernel,
        out_shape=out_shape,
        in_specs=in_specs,
        out_specs=out_specs,
        scratch_shapes=list(scratch),
        compiler_params=PARAMS,
        **options,
    )


def in_hbm(a):
    return pltpu.with_memory_space_constraint(a, pltpu.HBM)


def swap_cores(a):
    return lax.ppermute(a, "core", [(0, 1), (1, 0)])


def purify_call(flags, windows, other, cleared):
    return call(
        purify_kernel,
        bf16(4 * BS, 8 * BS),
        [ANY, VMEM, VMEM, HBM],
        HBM,
        [
            pltpu.SMEM((12, 24), jnp.int32),
            pltpu.VMEM((4, 5, BS, BS), jnp.float32),
            pltpu.VMEM((4, 5, BS, 2 * BS), jnp.bfloat16),
            pltpu.VMEM((4, BS, 8 * BS), jnp.bfloat16),
            pltpu.SemaphoreType.DMA((5,)),
        ],
        input_output_aliases={3: 0},
    )(flags, windows, other, cleared)


def body(built, build_order, p_pattern, q_pattern):
    parts = call(
        pick_kernel,
        bf16(CHIPS, 12, PART, BS),
        [HBM, HBM],
        scratch=[
            pltpu.SMEM((64,), jnp.int32),
            pltpu.VMEM((4, CHIPS, PART, 8 * BS), jnp.bfloat16),
            pltpu.SemaphoreType.DMA((5,)),
        ],
    )(in_hbm(build_order), in_hbm(built.reshape(4, CHIPS, PART, 8 * BS)))
    parts = lax.all_to_all(parts, ("x", "zl"), 0, 0, tiled=True).reshape(PARTS, PART, BS)
    found = call(
        edge_find_kernel, jax.ShapeDtypeStruct((10,), jnp.int32), [ANY] * 3, SMEM, SEARCH
    )(build_order, p_pattern, parts)
    both = (parts, swap_cores(parts))
    edge = call(edge_kernel, bf16(10, PART, BS), [SMEM, VMEM, VMEM])(found, *both)
    beside = lax.ppermute(edge, ("zl", "core", "yl", "zh"), to_groups())
    own = call(
        own_kernel, bf16(48, PART, BS), [ANY, ANY, VMEM, VMEM, ANY], scratch=SEARCH
    )(build_order, p_pattern, *both, edge)
    cleared = call(
        clear_kernel,
        pltpu.HBM((4 * BS, 8 * BS), jnp.bfloat16),
        [ANY],
        HBM,
        [pltpu.VMEM((BS, 8 * BS), jnp.bfloat16), pltpu.SemaphoreType.DMA((4,))],
    )(edge)
    windows = call(
        window_kernel,
        bf16(2 * CHIPS, WIN, PART, BS),
        [VMEM, VMEM, HBM],
        scratch=[pltpu.VMEM((2, WIDE, PART, BS), jnp.bfloat16)],
    )(beside, own, in_hbm(cleared))
    windows = lax.all_to_all(windows, ("x", "zl", "yh"), 0, 0, tiled=True)
    flags = call(
        flags_kernel,
        jax.ShapeDtypeStruct((12, 24), jnp.int32),
        [ANY, ANY],
        SMEM,
        [pltpu.SMEM((24, 64), jnp.int32), pltpu.SemaphoreType.DMA((3,))],
    )(q_pattern, windows)
    return purify_call(flags, windows, swap_cores(windows[:, SHARED:]), cleared)


def solution(mesh):
    fine = Mesh(mesh.devices.reshape(GRID), AXES)
    placed = (P(ROW, COL), P(), P(), P())
    return jax.shard_map(
        body, mesh=fine, in_specs=placed, out_specs=P(ROW, COL), check_vma=False
    )
```

```python
import functools

import jax
import jax.numpy as jnp
import numpy as np
from jax import lax
from jax.experimental import pallas as pl
from jax.experimental.pallas import tpu as pltpu
from jax.sharding import Mesh
from jax.sharding import PartitionSpec as P

BS = 128
GRID = (4, 2, 2, 2, 2, 2)
AXES = ("x", "zl", "core", "yh", "yl", "zh")
ROW = ("x", "zl", "core")
COL = ("yh", "yl", "zh")
CHIPS = 8
PART = BS // CHIPS
PARTS = CHIPS * 12
WIDE = 34
WIN = 28
SHARED = 18

VMEM = pl.BlockSpec(memory_space=pltpu.VMEM)
SMEM = pl.BlockSpec(memory_space=pltpu.SMEM)
ANY = pl.BlockSpec(memory_space=pl.ANY)
HBM = pl.BlockSpec(memory_space=pltpu.HBM)
PARAMS = pltpu.CompilerParams(vmem_limit_bytes=48 * 1024 * 1024)


def chip_index():
    return lax.axis_index("x") * 2 + lax.axis_index("zl")


def group_index():
    return lax.axis_index("yl") * 2 + lax.axis_index("zh")


def pick_kernel(order, built, out, order_s, built_v, sem):
    fetch = pltpu.make_async_copy(order, order_s, sem.at[4])
    fetch.start()
    copies = [pltpu.make_async_copy(built.at[k], built_v.at[k], sem.at[k]) for k in range(4)]
    for copy in copies:
        copy.start()
    fetch.wait()
    first = (chip_index() * 2 + lax.axis_index("core")) * 4
    zh = lax.axis_index("zh")
    for k in range(4):
        row = order_s[first + k]
        copies[k].wait()
        for d in range(3):
            col = lax.rem(row + d + 31, 8)
            at = pl.ds(pl.multiple_of(col * BS, BS), BS)
            for chip in range(0, CHIPS, 2):
                out[chip, 3 * k + d] = built_v[k, chip + zh, :, at]
                out[chip + 1, 3 * k + d] = built_v[k, chip + 1 - zh, :, at]


def search(tiles, order_in, pattern_in, order, pattern, inverse, sem):
    core = lax.axis_index("core")
    yh = lax.axis_index("yh")
    base = group_index() * 8
    copies = [pltpu.make_async_copy(order_in, order, sem.at[0])]
    for half in range(2):
        for n in tiles:
            rows = lax.rem(base + 8 * n + 24, 32) + 32 * half
            copies.append(
                pltpu.make_async_copy(
                    pattern_in.at[pl.ds(pl.multiple_of(rows, 8), 8)],
                    pattern.at[pl.ds(pl.multiple_of(24 * half + 8 * n, 8), 8)],
                    sem.at[len(copies)],
                )
            )
    for copy in copies:
        copy.start()
    copies[0].wait()
    for k in range(64):
        inverse[order[k]] = k
    for copy in copies[1:]:
        copy.wait()

    def find(half, n):
        bl, e = (n // 3, n % 3) if isinstance(n, int) else (lax.div(n, 3), lax.rem(n, 3))
        at = inverse[lax.rem(base + bl + e + 31, 32) + 32 * half]
        device = at // 4
        slot = (device // 2) * 12 + lax.rem(at, 4) * 3 + (2 - e)
        slot = jnp.where(lax.rem(device, 2) == core, slot, slot + PARTS)
        keep = pattern[24 * half + 7 + bl + e, base + bl + 32 * yh] != 0
        return jnp.where(keep, slot, 2 * PARTS)

    return find


SEARCH = [
    pltpu.SMEM((64,), jnp.int32),
    pltpu.SMEM((48, 64), jnp.int32),
    pltpu.SMEM((64,), jnp.int32),
    pltpu.SemaphoreType.DMA((7,)),
]


def edge_find_kernel(order_in, pattern_in, ready, out, *scratch):
    ahead = 1 - lax.axis_index("core")
    find = search((ahead, ahead + 1), order_in, pattern_in, *scratch)
    first = 19 * ahead
    for half in range(2):
        for n in range(5):
            out[5 * half + n] = find(half, first + n)


def take(at, mine, other):
    here = at < PARTS
    at_mine = jnp.where(here, at, 0)
    at_other = jnp.where(jnp.logical_and(at >= PARTS, at < 2 * PARTS), at - PARTS, 0)
    value = jnp.where(here, mine[at_mine], other[at_other])
    return jnp.where(at < 2 * PARTS, value, jnp.zeros_like(value))


def edge_kernel(found, mine, other, out):
    for n in range(10):
        out[n] = take(found[n], mine, other)


def own_kernel(order_in, pattern_in, mine, other, edge, out, *scratch):
    find = search(range(3), order_in, pattern_in, *scratch)
    for half in range(2):
        for n in range(24):
            out[24 * half + n] = take(find(half, n), mine, other)


def flags_kernel(pattern_in, ready, flags, pattern, sem):
    base = group_index() * 8
    copies = []
    for n in range(3):
        rows = lax.rem(base + 8 * n + 24, 32) + 32 * (chip_index() // 4)
        copies.append(
            pltpu.make_async_copy(
                pattern_in.at[pl.ds(pl.multiple_of(rows, 8), 8)],
                pattern.at[pl.ds(8 * n, 8)],
                sem.at[n],
            )
        )
        copies[-1].start()
    for copy in copies:
        copy.wait()
    for row in range(-2, 10):
        for col in range(max(-2, row - 2), min(9, row + 2) + 1):
            j = lax.rem(base + col + 32, 32)
            for half in range(2):
                flags[row + 2, 2 * (col + 2) + half] = pattern[8 + row, j + 32 * half]


def distance(chip):
    return lax.rem(chip - group_index() + 8, 4)


def window_kernel(beside, own, ready, out, wide):
    for half in range(2):
        wide[half, 0:5] = beside[5 * half : 5 * half + 5]
        wide[half, 5:29] = own[24 * half : 24 * half + 24]
        wide[half, 29:34] = beside[5 * half : 5 * half + 5]
    core = lax.axis_index("core")
    for chip in range(CHIPS):
        away = distance(chip)
        right, left = away == 1, away == 3
        edge = jnp.logical_or(right, left)
        pick = lambda r, l, other: jnp.where(right, r, jnp.where(left, l, other))
        alone = pick(24, 5, 3 + 19 * core)
        for half in range(2):
            at = 2 * chip + half
            for h in range(2):
                out[at, 9 * h : 9 * h + 9] = wide[h, pl.ds(alone, 9)]
                shared = wide[jnp.where(edge, h, core), pl.ds(pick(29, 0, 12 + 5 * h), 5)]
                out[at, SHARED + 5 * h : SHARED + 5 * h + 5] = shared


def clear_kernel(ready, out, zeros, sem):
    zeros[...] = jnp.zeros_like(zeros)
    copies = [
        pltpu.make_async_copy(zeros, out.at[pl.ds(k * BS, BS)], sem.at[k]) for k in range(4)
    ]
    for copy in copies:
        copy.start()
    for copy in copies:
        copy.wait()


def purify_kernel(flags_in, mine, other, cleared, out, flags, squares, rounded, result, sem):
    fetch = pltpu.make_async_copy(flags_in, flags, sem.at[4])
    fetch.start()
    core = lax.axis_index("core")
    yh = lax.axis_index("yh")
    zh = lax.axis_index("zh")
    chip = chip_index()
    away = distance(chip)
    row_half = chip // 4

    def dot(a, b):
        return jnp.dot(a, b, preferred_element_type=jnp.float32)

    def block(ref, n, half):
        rows = [ref[2 * (p + zh if p % 2 == 0 else p - zh) + half, n] for p in range(CHIPS)]
        return jnp.concatenate(rows, 0)

    def kept(row, col, half):
        return flags[row + 2, 2 * (col + 2) + half] != 0

    def work(locate, rows, results):
        def half_block(f, h, half):
            n = locate(f, h)
            return block(mine, n, half) if n >= 0 else block(other, n + 10, half)

        def number(row, col):
            return 2 * col + row + 6

        def column(row, col, half):
            return jnp.concatenate([half_block(number(row, col), h, half) for h in range(2)], 0)

        def whole(row, col):
            return jnp.concatenate([column(row, col, half) for half in range(2)], 1)

        def left(row, col):
            f = number(row, col)
            low, high = locate(f, 0), locate(f, 1)
            if low >= 0 and high >= 0:
                n = low + row_half * (high - low)
                return jnp.concatenate([block(mine, n, half) for half in range(2)], 1)
            parts = [
                jnp.where(row_half == 0, half_block(f, 0, half), half_block(f, 1, half))
                for half in range(2)
            ]
            return jnp.concatenate(parts, 1)

        near = lambda a, b, d=1: abs(a - b) <= d
        span = range(-2, 10)
        cols = {a: sorted({k for b, j in results if b == a for k in span if near(k, j) and near(k, a, 2)}) for a in rows}
        copies = []
        for r_at, a in enumerate(rows):
            first = cols[a][0]
            for k in cols[a]:
                ls = [l for l in span if near(l, a) and near(l, k)]
                total = dot(
                    jnp.concatenate([left(a, l) for l in ls], 1),
                    jnp.concatenate([whole(l, k) for l in ls], 0),
                )
                if r_at == 0 and k == first:
                    fetch.wait()
                parts = []
                for half in range(2):
                    part = total[:, half * BS : (half + 1) * BS]
                    parts.append(jnp.where(kept(a, k, half), part, jnp.zeros_like(part)))
                squares[r_at, k - first] = jnp.where(yh == 0, parts[0], parts[1])
                rounded[r_at, k - first] = jnp.concatenate(parts, 1).astype(jnp.bfloat16)
            spots = [(j, r, c) for (b, j), (r, c) in results.items() if b == a]
            js = [j for j, _, _ in spots]
            totals = {}
            for pair in [js[n : n + 2] for n in range(0, len(js), 2)]:
                ks = [k for k in cols[a] if any(near(k, j) for j in pair)]
                rights = [
                    [column(k, j, yh) if near(k, j) else jnp.zeros((2 * BS, BS), jnp.bfloat16) for j in pair]
                    for k in ks
                ]
                total = dot(
                    jnp.concatenate([rounded[r_at, k - first] for k in ks], 1),
                    jnp.concatenate([jnp.concatenate(right, 1) for right in rights], 0),
                )
                for n, j in enumerate(pair):
                    totals[j] = total[:, n * BS : (n + 1) * BS]
            for j, r, c in spots:
                value = 3.0 * squares[r_at, j - first] - 2.0 * totals[j]
                value = jnp.where(kept(a, j, yh), value, jnp.zeros_like(value))
                result[r, :, c * BS : (c + 1) * BS] = value.astype(jnp.bfloat16)
            r = spots[0][1]
            low, high = min(c for *_, c in spots) * BS, (max(c for *_, c in spots) + 1) * BS
            copies.append(
                pltpu.make_async_copy(
                    result.at[r, :, low:high],
                    out.at[pl.ds(r * BS, BS), low:high],
                    sem.at[r_at],
                )
            )
            copies[-1].start()
        for copy in copies:
            copy.wait()

    def low(f, h):
        return f - 3 + 9 * h if f < 12 else SHARED + f - 12 if h == 0 else f - 22

    def high(f, h):
        return f - 22 + 9 * h if f > 21 else SHARED + f - 12 if h == 1 else f - 22

    def beyond(f, h):
        return f - 24 + 9 * h if f < 29 else f - 39 + 5 * h

    def before(f, h):
        return f - 5 + 9 * h if f > 4 else f - 10 + 5 * h

    for u, locate in enumerate((low, high)):

        @pl.when(jnp.logical_and(away == 0, core == u))
        def _(u=u, locate=locate):
            rows = list(range(4 * u, 4 * u + 4))
            spots = [(a, j) for a in rows for j in range(a - 2, a + 3) if 0 <= j < 8]
            work(locate, rows, {(a, j): (a - 4 * u, j) for a, j in spots})

    @pl.when(jnp.logical_and(away == 1, core == 0))
    def _():
        work(beyond, [8, 9], {(8, 6): (0, 6), (8, 7): (0, 7), (9, 7): (1, 7)})

    last = jnp.logical_and(away == 3, core == 1)
    near_one = jnp.logical_or(jnp.logical_and(away == 1, core == 0), last)

    @pl.when(jnp.logical_and(away != 0, jnp.logical_not(near_one)))
    def _():
        fetch.wait()

    @pl.when(last)
    def _():
        work(before, [-1, -2], {(-1, 1): (3, 1), (-1, 0): (3, 0), (-2, 0): (2, 0)})


def to_groups():
    index = lambda zl, core, g: (zl * 2 + core) * 4 + g % 4
    return [
        (index(zl, core, g), index(1 - zl, core, g + (3 if core else 1)))
        for zl in range(2)
        for core in range(2)
        for g in range(4)
    ]


def bf16(*shape):
    return jax.ShapeDtypeStruct(shape, jnp.bfloat16)


def call(kernel, out_shape, in_specs, out_specs=VMEM, scratch=(), **options):
    if isinstance(out_shape, list) and not isinstance(out_specs, list):
        out_specs = [out_specs] * len(out_shape)
    return pl.pallas_call(
        kernel,
        out_shape=out_shape,
        in_specs=in_specs,
        out_specs=out_specs,
        scratch_shapes=list(scratch),
        compiler_params=PARAMS,
        **options,
    )


def in_hbm(a):
    return pltpu.with_memory_space_constraint(a, pltpu.HBM)


def swap_cores(a):
    return lax.ppermute(a, "core", [(0, 1), (1, 0)])


def purify_call(flags, windows, other, cleared):
    return call(
        purify_kernel,
        bf16(4 * BS, 8 * BS),
        [ANY, VMEM, VMEM, HBM],
        HBM,
        [
            pltpu.SMEM((12, 24), jnp.int32),
            pltpu.VMEM((4, 5, BS, BS), jnp.float32),
            pltpu.VMEM((4, 5, BS, 2 * BS), jnp.bfloat16),
            pltpu.VMEM((4, BS, 8 * BS), jnp.bfloat16),
            pltpu.SemaphoreType.DMA((5,)),
        ],
        input_output_aliases={3: 0},
    )(flags, windows, other, cleared)


def body(built, build_order, p_pattern, q_pattern):
    parts = call(
        pick_kernel,
        bf16(CHIPS, 12, PART, BS),
        [HBM, HBM],
        scratch=[
            pltpu.SMEM((64,), jnp.int32),
            pltpu.VMEM((4, CHIPS, PART, 8 * BS), jnp.bfloat16),
            pltpu.SemaphoreType.DMA((5,)),
        ],
    )(in_hbm(build_order), in_hbm(built.reshape(4, CHIPS, PART, 8 * BS)))
    parts = lax.all_to_all(parts, ("x", "zl"), 0, 0, tiled=True).reshape(PARTS, PART, BS)
    found = call(
        edge_find_kernel, jax.ShapeDtypeStruct((10,), jnp.int32), [ANY] * 3, SMEM, SEARCH
    )(build_order, p_pattern, parts)
    both = (parts, swap_cores(parts))
    edge = call(edge_kernel, bf16(10, PART, BS), [SMEM, VMEM, VMEM])(found, *both)
    beside = lax.ppermute(edge, ("zl", "core", "yl", "zh"), to_groups())
    own = call(
        own_kernel, bf16(48, PART, BS), [ANY, ANY, VMEM, VMEM, ANY], scratch=SEARCH
    )(build_order, p_pattern, *both, edge)
    cleared = call(
        clear_kernel,
        pltpu.HBM((4 * BS, 8 * BS), jnp.bfloat16),
        [ANY],
        HBM,
        [pltpu.VMEM((BS, 8 * BS), jnp.bfloat16), pltpu.SemaphoreType.DMA((4,))],
    )(edge)
    windows = call(
        window_kernel,
        bf16(2 * CHIPS, WIN, PART, BS),
        [VMEM, VMEM, HBM],
        scratch=[pltpu.VMEM((2, WIDE, PART, BS), jnp.bfloat16)],
    )(beside, own, in_hbm(cleared))
    windows = lax.all_to_all(windows, ("x", "zl", "yh"), 0, 0, tiled=True)
    flags = call(
        flags_kernel,
        jax.ShapeDtypeStruct((12, 24), jnp.int32),
        [ANY, ANY],
        SMEM,
        [pltpu.SMEM((24, 64), jnp.int32), pltpu.SemaphoreType.DMA((3,))],
    )(q_pattern, windows)
    return purify_call(flags, windows, swap_cores(windows[:, SHARED:]), cleared)


def solution(mesh):
    fine = Mesh(mesh.devices.reshape(GRID), AXES)
    placed = (P(ROW, COL), P(), P(), P())
    return jax.shard_map(
        body, mesh=fine, in_specs=placed, out_specs=P(ROW, COL), check_vma=False
    )
```

```python
import functools

import jax
import jax.numpy as jnp
import numpy as np
from jax import lax
from jax.experimental import pallas as pl
from jax.experimental.pallas import tpu as pltpu
from jax.sharding import Mesh
from jax.sharding import PartitionSpec as P

BS = 128
GRID = (4, 2, 2, 2, 2, 2)
AXES = ("x", "zl", "core", "yh", "yl", "zh")
ROW = ("x", "zl", "core")
COL = ("yh", "yl", "zh")
CHIPS = 8
PART = BS // CHIPS
PARTS = CHIPS * 12
WIDE = 34
WIN = 28
SHARED = 18

VMEM = pl.BlockSpec(memory_space=pltpu.VMEM)
SMEM = pl.BlockSpec(memory_space=pltpu.SMEM)
ANY = pl.BlockSpec(memory_space=pl.ANY)
HBM = pl.BlockSpec(memory_space=pltpu.HBM)
PARAMS = pltpu.CompilerParams(vmem_limit_bytes=48 * 1024 * 1024)


def chip_index():
    return lax.axis_index("x") * 2 + lax.axis_index("zl")


def group_index():
    return lax.axis_index("yl") * 2 + lax.axis_index("zh")


def pick_kernel(order, built, out, order_s, built_v, sem):
    fetch = pltpu.make_async_copy(order, order_s, sem.at[4])
    fetch.start()
    copies = [pltpu.make_async_copy(built.at[k], built_v.at[k], sem.at[k]) for k in range(4)]
    for copy in copies:
        copy.start()
    fetch.wait()
    first = (chip_index() * 2 + lax.axis_index("core")) * 4
    zh = lax.axis_index("zh")
    for k in range(4):
        row = order_s[first + k]
        copies[k].wait()
        for d in range(3):
            col = lax.rem(row + d + 31, 8)
            at = pl.ds(pl.multiple_of(col * BS, BS), BS)
            for chip in range(0, CHIPS, 2):
                out[chip, 3 * k + d] = built_v[k, chip + zh, :, at]
                out[chip + 1, 3 * k + d] = built_v[k, chip + 1 - zh, :, at]


def search(tiles, order_in, pattern_in, order, pattern, inverse, sem):
    core = lax.axis_index("core")
    yh = lax.axis_index("yh")
    base = group_index() * 8
    copies = [pltpu.make_async_copy(order_in, order, sem.at[0])]
    for half in range(2):
        for n in tiles:
            rows = lax.rem(base + 8 * n + 24, 32) + 32 * half
            copies.append(
                pltpu.make_async_copy(
                    pattern_in.at[pl.ds(pl.multiple_of(rows, 8), 8)],
                    pattern.at[pl.ds(pl.multiple_of(24 * half + 8 * n, 8), 8)],
                    sem.at[len(copies)],
                )
            )
    for copy in copies:
        copy.start()
    copies[0].wait()
    for k in range(64):
        inverse[order[k]] = k
    for copy in copies[1:]:
        copy.wait()

    def find(half, n):
        bl, e = (n // 3, n % 3) if isinstance(n, int) else (lax.div(n, 3), lax.rem(n, 3))
        at = inverse[lax.rem(base + bl + e + 31, 32) + 32 * half]
        device = at // 4
        slot = (device // 2) * 12 + lax.rem(at, 4) * 3 + (2 - e)
        slot = jnp.where(lax.rem(device, 2) == core, slot, slot + PARTS)
        keep = pattern[24 * half + 7 + bl + e, base + bl + 32 * yh] != 0
        return jnp.where(keep, slot, 2 * PARTS)

    return find


SEARCH = [
    pltpu.SMEM((64,), jnp.int32),
    pltpu.SMEM((48, 64), jnp.int32),
    pltpu.SMEM((64,), jnp.int32),
    pltpu.SemaphoreType.DMA((7,)),
]


def edge_find_kernel(order_in, pattern_in, ready, out, *scratch):
    ahead = 1 - lax.axis_index("core")
    find = search((ahead, ahead + 1), order_in, pattern_in, *scratch)
    first = 19 * ahead
    for half in range(2):
        for n in range(5):
            out[5 * half + n] = find(half, first + n)


def take(at, mine, other):
    here = at < PARTS
    at_mine = jnp.where(here, at, 0)
    at_other = jnp.where(jnp.logical_and(at >= PARTS, at < 2 * PARTS), at - PARTS, 0)
    value = jnp.where(here, mine[at_mine], other[at_other])
    return jnp.where(at < 2 * PARTS, value, jnp.zeros_like(value))


def edge_kernel(found, mine, other, out):
    for n in range(10):
        out[n] = take(found[n], mine, other)


def own_kernel(order_in, pattern_in, mine, other, edge, out, *scratch):
    find = search(range(3), order_in, pattern_in, *scratch)
    for half in range(2):
        for n in range(24):
            out[24 * half + n] = take(find(half, n), mine, other)


def flags_kernel(pattern_in, ready, flags, pattern, sem):
    base = group_index() * 8
    copies = []
    for n in range(3):
        rows = lax.rem(base + 8 * n + 24, 32) + 32 * (chip_index() // 4)
        copies.append(
            pltpu.make_async_copy(
                pattern_in.at[pl.ds(pl.multiple_of(rows, 8), 8)],
                pattern.at[pl.ds(8 * n, 8)],
                sem.at[n],
            )
        )
        copies[-1].start()
    for copy in copies:
        copy.wait()
    for row in range(-2, 10):
        for col in range(max(-2, row - 2), min(9, row + 2) + 1):
            j = lax.rem(base + col + 32, 32)
            for half in range(2):
                flags[row + 2, 2 * (col + 2) + half] = pattern[8 + row, j + 32 * half]


def distance(chip):
    return lax.rem(chip - group_index() + 8, 4)


def window_kernel(beside, own, ready, out, wide):
    for half in range(2):
        wide[half, 0:5] = beside[5 * half : 5 * half + 5]
        wide[half, 5:29] = own[24 * half : 24 * half + 24]
        wide[half, 29:34] = beside[5 * half : 5 * half + 5]
    core = lax.axis_index("core")
    for chip in range(CHIPS):
        away = distance(chip)
        right, left = away == 1, away == 3
        edge = jnp.logical_or(right, left)
        pick = lambda r, l, other: jnp.where(right, r, jnp.where(left, l, other))
        alone = pick(24, 5, 3 + 19 * core)
        for half in range(2):
            at = 2 * chip + half
            for h in range(2):
                out[at, 9 * h : 9 * h + 9] = wide[h, pl.ds(alone, 9)]
                shared = wide[jnp.where(edge, h, core), pl.ds(pick(29, 0, 12 + 5 * h), 5)]
                out[at, SHARED + 5 * h : SHARED + 5 * h + 5] = shared


def clear_kernel(ready, out, zeros, sem):
    zeros[...] = jnp.zeros_like(zeros)
    copies = [
        pltpu.make_async_copy(zeros, out.at[pl.ds(k * BS, BS)], sem.at[k]) for k in range(4)
    ]
    for copy in copies:
        copy.start()
    for copy in copies:
        copy.wait()


def purify_kernel(flags_in, mine, other, cleared, out, flags, squares, rounded, result, sem):
    fetch = pltpu.make_async_copy(flags_in, flags, sem.at[4])
    fetch.start()
    core = lax.axis_index("core")
    yh = lax.axis_index("yh")
    zh = lax.axis_index("zh")
    chip = chip_index()
    away = distance(chip)
    row_half = chip // 4

    def dot(a, b):
        return jnp.dot(a, b, preferred_element_type=jnp.float32)

    def block(ref, n, half):
        rows = [ref[2 * (p + zh if p % 2 == 0 else p - zh) + half, n] for p in range(CHIPS)]
        return jnp.concatenate(rows, 0)

    def kept(row, col, half):
        return flags[row + 2, 2 * (col + 2) + half] != 0

    def work(locate, rows, results):
        def half_block(f, h, half):
            n = locate(f, h)
            return block(mine, n, half) if n >= 0 else block(other, n + 10, half)

        def number(row, col):
            return 2 * col + row + 6

        def column(row, col, half):
            return jnp.concatenate([half_block(number(row, col), h, half) for h in range(2)], 0)

        def whole(row, col):
            return jnp.concatenate([column(row, col, half) for half in range(2)], 1)

        def left(row, col):
            f = number(row, col)
            low, high = locate(f, 0), locate(f, 1)
            if low >= 0 and high >= 0:
                n = low + row_half * (high - low)
                return jnp.concatenate([block(mine, n, half) for half in range(2)], 1)
            parts = [
                jnp.where(row_half == 0, half_block(f, 0, half), half_block(f, 1, half))
                for half in range(2)
            ]
            return jnp.concatenate(parts, 1)

        near = lambda a, b, d=1: abs(a - b) <= d
        span = range(-2, 10)
        cols = {a: sorted({k for b, j in results if b == a for k in span if near(k, j) and near(k, a, 2)}) for a in rows}
        copies = []
        for r_at, a in enumerate(rows):
            first = cols[a][0]
            for k in cols[a]:
                ls = [l for l in span if near(l, a) and near(l, k)]
                total = dot(
                    jnp.concatenate([left(a, l) for l in ls], 1),
                    jnp.concatenate([whole(l, k) for l in ls], 0),
                )
                if r_at == 0 and k == first:
                    fetch.wait()
                parts = []
                for half in range(2):
                    part = total[:, half * BS : (half + 1) * BS]
                    parts.append(jnp.where(kept(a, k, half), part, jnp.zeros_like(part)))
                squares[r_at, k - first] = jnp.where(yh == 0, parts[0], parts[1])
                rounded[r_at, k - first] = jnp.concatenate(parts, 1).astype(jnp.bfloat16)
            spots = [(j, r, c) for (b, j), (r, c) in results.items() if b == a]
            js = [j for j, _, _ in spots]
            totals = {}
            for pair in [js[n : n + 2] for n in range(0, len(js), 2)]:
                ks = [k for k in cols[a] if any(near(k, j) for j in pair)]
                rights = [
                    [column(k, j, yh) if near(k, j) else jnp.zeros((2 * BS, BS), jnp.bfloat16) for j in pair]
                    for k in ks
                ]
                total = dot(
                    jnp.concatenate([rounded[r_at, k - first] for k in ks], 1),
                    jnp.concatenate([jnp.concatenate(right, 1) for right in rights], 0),
                )
                for n, j in enumerate(pair):
                    totals[j] = total[:, n * BS : (n + 1) * BS]
            for j, r, c in spots:
                value = 3.0 * squares[r_at, j - first] - 2.0 * totals[j]
                value = jnp.where(kept(a, j, yh), value, jnp.zeros_like(value))
                result[r, :, c * BS : (c + 1) * BS] = value.astype(jnp.bfloat16)
            r = spots[0][1]
            low, high = min(c for *_, c in spots) * BS, (max(c for *_, c in spots) + 1) * BS
            copies.append(
                pltpu.make_async_copy(
                    result.at[r, :, low:high],
                    out.at[pl.ds(r * BS, BS), low:high],
                    sem.at[r_at],
                )
            )
            copies[-1].start()
        for copy in copies:
            copy.wait()

    def low(f, h):
        return f - 3 + 9 * h if f < 12 else SHARED + f - 12 if h == 0 else f - 22

    def high(f, h):
        return f - 22 + 9 * h if f > 21 else SHARED + f - 12 if h == 1 else f - 22

    def beyond(f, h):
        return f - 24 + 9 * h if f < 29 else f - 39 + 5 * h

    def before(f, h):
        return f - 5 + 9 * h if f > 4 else f - 10 + 5 * h

    for u, locate in enumerate((low, high)):

        @pl.when(jnp.logical_and(away == 0, core == u))
        def _(u=u, locate=locate):
            rows = list(range(4, 8) if u else range(3, -1, -1))
            spots = [(a, j) for a in rows for j in range(a - 2, a + 3) if 0 <= j < 8]
            work(locate, rows, {(a, j): (a - 4 * u, j) for a, j in spots})

    @pl.when(jnp.logical_and(away == 1, core == 0))
    def _():
        work(beyond, [8, 9], {(8, 6): (0, 6), (8, 7): (0, 7), (9, 7): (1, 7)})

    last = jnp.logical_and(away == 3, core == 1)
    near_one = jnp.logical_or(jnp.logical_and(away == 1, core == 0), last)

    @pl.when(jnp.logical_and(away != 0, jnp.logical_not(near_one)))
    def _():
        fetch.wait()

    @pl.when(last)
    def _():
        work(before, [-1, -2], {(-1, 1): (3, 1), (-1, 0): (3, 0), (-2, 0): (2, 0)})


def to_groups():
    index = lambda zl, core, g: (zl * 2 + core) * 4 + g % 4
    return [
        (index(zl, core, g), index(1 - zl, core, g + (3 if core else 1)))
        for zl in range(2)
        for core in range(2)
        for g in range(4)
    ]


def bf16(*shape):
    return jax.ShapeDtypeStruct(shape, jnp.bfloat16)


def call(kernel, out_shape, in_specs, out_specs=VMEM, scratch=(), **options):
    if isinstance(out_shape, list) and not isinstance(out_specs, list):
        out_specs = [out_specs] * len(out_shape)
    return pl.pallas_call(
        kernel,
        out_shape=out_shape,
        in_specs=in_specs,
        out_specs=out_specs,
        scratch_shapes=list(scratch),
        compiler_params=PARAMS,
        **options,
    )


def in_hbm(a):
    return pltpu.with_memory_space_constraint(a, pltpu.HBM)


def swap_cores(a):
    return lax.ppermute(a, "core", [(0, 1), (1, 0)])


def purify_call(flags, windows, other, cleared):
    return call(
        purify_kernel,
        bf16(4 * BS, 8 * BS),
        [ANY, VMEM, VMEM, HBM],
        HBM,
        [
            pltpu.SMEM((12, 24), jnp.int32),
            pltpu.VMEM((4, 5, BS, BS), jnp.float32),
            pltpu.VMEM((4, 5, BS, 2 * BS), jnp.bfloat16),
            pltpu.VMEM((4, BS, 8 * BS), jnp.bfloat16),
            pltpu.SemaphoreType.DMA((5,)),
        ],
        input_output_aliases={3: 0},
    )(flags, windows, other, cleared)


def body(built, build_order, p_pattern, q_pattern):
    parts = call(
        pick_kernel,
        bf16(CHIPS, 12, PART, BS),
        [HBM, HBM],
        scratch=[
            pltpu.SMEM((64,), jnp.int32),
            pltpu.VMEM((4, CHIPS, PART, 8 * BS), jnp.bfloat16),
            pltpu.SemaphoreType.DMA((5,)),
        ],
    )(in_hbm(build_order), in_hbm(built.reshape(4, CHIPS, PART, 8 * BS)))
    parts = lax.all_to_all(parts, ("x", "zl"), 0, 0, tiled=True).reshape(PARTS, PART, BS)
    found = call(
        edge_find_kernel, jax.ShapeDtypeStruct((10,), jnp.int32), [ANY] * 3, SMEM, SEARCH
    )(build_order, p_pattern, parts)
    both = (parts, swap_cores(parts))
    edge = call(edge_kernel, bf16(10, PART, BS), [SMEM, VMEM, VMEM])(found, *both)
    beside = lax.ppermute(edge, ("zl", "core", "yl", "zh"), to_groups())
    own = call(
        own_kernel, bf16(48, PART, BS), [ANY, ANY, VMEM, VMEM, ANY], scratch=SEARCH
    )(build_order, p_pattern, *both, edge)
    cleared = call(
        clear_kernel,
        pltpu.HBM((4 * BS, 8 * BS), jnp.bfloat16),
        [ANY],
        HBM,
        [pltpu.VMEM((BS, 8 * BS), jnp.bfloat16), pltpu.SemaphoreType.DMA((4,))],
    )(edge)
    windows = call(
        window_kernel,
        bf16(2 * CHIPS, WIN, PART, BS),
        [VMEM, VMEM, HBM],
        scratch=[pltpu.VMEM((2, WIDE, PART, BS), jnp.bfloat16)],
    )(beside, own, in_hbm(cleared))
    windows = lax.all_to_all(windows, ("x", "zl", "yh"), 0, 0, tiled=True)
    flags = call(
        flags_kernel,
        jax.ShapeDtypeStruct((12, 24), jnp.int32),
        [ANY, ANY],
        SMEM,
        [pltpu.SMEM((24, 64), jnp.int32), pltpu.SemaphoreType.DMA((3,))],
    )(q_pattern, windows)
    return purify_call(flags, windows, swap_cores(windows[:, SHARED:]), cleared)


def solution(mesh):
    fine = Mesh(mesh.devices.reshape(GRID), AXES)
    placed = (P(ROW, COL), P(), P(), P())
    return jax.shard_map(
        body, mesh=fine, in_specs=placed, out_specs=P(ROW, COL), check_vma=False
    )
```
